32 devices in a mesh: groups: 2 (over y), tok: 16 (over z, x, core).
Axes of the slice: x: 2, y: 2, z: 4, core: 2. Of those that a mesh axis runs over, the one named last changes fastest.
Arguments:
- queries: bfloat16 [2048, 2048], P(('groups', 'tok')), parts along dimension 0, may hold values from -256 to 256, as said below
- fresh_keys: bfloat16 [2048, 2048], P(('groups', 'tok')), parts along dimension 0, may hold values from -6 to 6, as said below
- fresh_values: bfloat16 [2048, 2048], P(('groups', 'tok')), parts along dimension 0, may hold values from -6 to 6
- stale_keys: bfloat16 [2048, 2048], P(('groups', 'tok')), parts along dimension 0, may hold values from -6 to 6
- stale_values: bfloat16 [2048, 2048], P(('groups', 'tok')), parts along dimension 0, may hold values from -6 to 6
- patch_starts: int32 [32], P('groups'), parts along dimension 0, may hold values from 0 to 1023, as said below
- order_starts: int32 [32], P('groups'), parts along dimension 0, may hold values from 0 to 1023, as said below
Outputs:
- attended: bfloat16 [2048, 2048], P(('groups', 'tok')), parts along dimension 0
The draws below stay inside these ranges and needn't reach their ends.
There are 2 independent parts, one for each index of `groups`. The reference program is written for one: setup_inputs(seed, part) draws one part's arguments, and reference() takes and returns one part's arrays. A program takes and returns all parts, laid end to end along the dimension named above; each array names one. Nothing has to cross between parts.
Inputs may be any that keep to these rules, and one draw needn't show every extreme that they name: `patch_starts`: strictly increasing; the first entry is 0. `order_starts`: the entries of patch_starts, each once, in processing order. `queries`: entries are finite. `fresh_keys`: entries are finite.
All inputs are finite; a program needn't handle non-finite values.
Results may differ from the reference program's by a relative error of at most 0.0049.
Values may be sent and summed in bfloat16 or wider, within the bound.
No kernel may reach another device: no remote copies, remote signals or barrier semaphores. Data moves between devices by JAX's collectives and lax.ppermute only.
A program may use at most 128 MiB of HBM per device.

```python
import math
import jax
import jax.numpy as jnp
from jax import lax

HEADS = 16
HEAD_DIM = 128
PATCHES = 16
TOKENS = 1024


def shared_keys(key):
    draws = jax.random.normal(jax.random.fold_in(key, 11), (TOKENS, HEADS * HEAD_DIM), jnp.float32)
    return jnp.clip(draws, -6.0, 6.0)


def draw_fresh_keys(key, part):
    return shared_keys(key).astype(jnp.bfloat16)


def draw_queries(key, part):
    base_key = jax.random.fold_in(key, 23)
    draws = jax.random.normal(base_key, (TOKENS, HEADS * HEAD_DIM), jnp.float32)
    return (3.0 * jnp.clip(draws, -4.0, 4.0)).astype(jnp.bfloat16)


def patch_layout(key):
    cut_points = jax.random.permutation(jax.random.fold_in(key, 5), TOKENS - 1)[:PATCHES - 1] + 1
    starts = jnp.concatenate([jnp.zeros((1,), jnp.int32), jnp.sort(cut_points.astype(jnp.int32))])
    ordering = jax.random.permutation(jax.random.fold_in(key, 6), PATCHES)
    return (starts, starts[ordering])


def draw_patch_starts(key, part):
    return patch_layout(key)[0].astype(jnp.int32)


def draw_order_starts(key, part):
    return patch_layout(key)[1].astype(jnp.int32)


def levels(key, extent, pieces, low, largest):
    def one(axis_at, parts):
        heights = jax.random.uniform(jax.random.fold_in(jax.random.fold_in(key, 6), axis_at), (parts,), jnp.float32, low / len(pieces), largest / len(pieces))
        return jnp.repeat(jnp.exp(heights), extent[axis_at] // parts).reshape((-1,) + (1,) * (len(extent) - axis_at - 1))

    loudness = one(*pieces[0])
    for cut in pieces[1:]:
        loudness = loudness * one(*cut)
    return loudness


def noise(rng, extent, deviation, reach, shards=(), kind=jnp.bfloat16):
    level = levels(rng, extent, shards, -0.22, 0.18) if shards else 1.0
    drawn = jax.random.normal(rng, extent, jnp.float32) * deviation * level
    return jnp.minimum(jnp.maximum(drawn, -reach), reach).astype(kind)


def setup_inputs(seed: int = 0, part: int = 0) -> dict:
    splits = jax.random.split(jax.random.key(seed), 8)
    part_keys = jax.random.split(jax.random.fold_in(splits[7], part), 8)
    queries = draw_queries(jax.random.fold_in(jax.random.fold_in(splits[7], part), 71), part)
    fresh_keys = draw_fresh_keys(jax.random.fold_in(jax.random.fold_in(splits[7], part), 71), part)
    fresh_values = noise(part_keys[2], (TOKENS, HEADS * HEAD_DIM), 1.0, 6.0, ((0, 16),))
    stale_keys = noise(part_keys[3], (TOKENS, HEADS * HEAD_DIM), 1.0, 6.0, ((0, 16),))
    stale_values = noise(part_keys[4], (TOKENS, HEADS * HEAD_DIM), 1.0, 6.0, ((0, 16),))
    patch_starts = draw_patch_starts(jax.random.fold_in(jax.random.fold_in(splits[7], part), 71), part)
    order_starts = draw_order_starts(jax.random.fold_in(jax.random.fold_in(splits[7], part), 71), part)
    return {"queries": queries, "fresh_keys": fresh_keys, "fresh_values": fresh_values, "stale_keys": stale_keys, "stale_values": stale_values, "patch_starts": patch_starts, "order_starts": order_starts}


def token_ranks(positions, patch_starts, order_starts):
    patch_count = patch_starts.shape[0]
    slot_ids = jnp.arange(patch_count, dtype=jnp.int32)
    patch_of = lax.optimization_barrier(jnp.sum((patch_starts[None, :] <= positions[:, None]).astype(jnp.int32), axis=1)) - 1
    matches = (order_starts[:, None] == patch_starts[None, :]).astype(jnp.int32)
    rank_of = lax.optimization_barrier(jnp.sum(matches * slot_ids[:, None], axis=0))
    one_hot = (patch_of[:, None] == slot_ids[None, :]).astype(jnp.int32)
    return lax.optimization_barrier(jnp.sum(one_hot * rank_of[None, :], axis=1))

def attend_block(query_block, query_rank, key_stack, key_rank):
    dims = (((1,), (1,)), ((), ()))
    score_scale = 1.0 / math.sqrt(query_block.shape[-1])
    fresh_scores = lax.dot_general(query_block, key_stack[0], dims, preferred_element_type=jnp.float32) * score_scale
    stale_scores = lax.dot_general(query_block, key_stack[2], dims, preferred_element_type=jnp.float32) * score_scale
    fresh_ok = key_rank[None, :] <= query_rank[:, None]
    fresh_scores = jnp.where(fresh_ok, fresh_scores, -jnp.inf)
    stale_scores = jnp.where(fresh_ok, -jnp.inf, stale_scores)
    row_max = jnp.maximum(lax.optimization_barrier(jnp.max(fresh_scores, axis=1)), lax.optimization_barrier(jnp.max(stale_scores, axis=1)))[:, None]
    fresh_exp = jnp.exp(fresh_scores - row_max)
    stale_exp = jnp.exp(stale_scores - row_max)
    row_total = lax.optimization_barrier(jnp.sum(fresh_exp, axis=1, keepdims=True)) + lax.optimization_barrier(jnp.sum(stale_exp, axis=1, keepdims=True))
    fresh_probs = (fresh_exp / row_total).astype(jnp.bfloat16)
    stale_probs = (stale_exp / row_total).astype(jnp.bfloat16)
    mixed = jnp.dot(fresh_probs, key_stack[1], preferred_element_type=jnp.float32)
    mixed = mixed + jnp.dot(stale_probs, key_stack[3], preferred_element_type=jnp.float32)
    return mixed.astype(jnp.bfloat16)

def attend_rows(query_rows, query_rank, key_stack, key_rank):
    row_count = query_rows.shape[0]
    block_rows = 512 if row_count % 512 == 0 else row_count
    blocks = row_count // block_rows

    def one_block(inputs):
        return attend_block(inputs[0], inputs[1], key_stack, key_rank)
    result = lax.map(one_block, (query_rows.reshape(blocks, block_rows, query_rows.shape[1]), query_rank.reshape(blocks, block_rows)))
    return result.reshape(row_count, query_rows.shape[1])

def reference(queries, fresh_keys, fresh_values, stale_keys, stale_values, patch_starts, order_starts):
    token_count = queries.shape[0]
    positions = jnp.arange(token_count, dtype=jnp.int32)
    ranks = token_ranks(positions, patch_starts, order_starts)

    def by_head(array):
        return array.reshape(token_count, HEADS, HEAD_DIM).transpose(1, 0, 2)
    stacked = jnp.stack([by_head(fresh_keys), by_head(fresh_values), by_head(stale_keys), by_head(stale_values)], axis=1)

    def one_head(inputs):
        return attend_rows(inputs[0], ranks, inputs[1], ranks)
    attended = lax.map(one_head, (by_head(queries), stacked))
    return attended.transpose(1, 0, 2).reshape(token_count, HEADS * HEAD_DIM)
```

```python
import functools
import math

import jax
import jax.numpy as jnp
from jax import lax
from jax.experimental import pallas as pl
from jax.experimental.pallas import tpu as pltpu
from jax.sharding import PartitionSpec as P

HEADS = 16
HEAD_DIM = 128
CORES = 2
STAT_ROWS = 16
STAT_TERMS = 4
CHUNK = 4
VMEM_LIMIT = 48 * 1024 * 1024


def token_ranks(positions, patch_starts, order_starts):
    patch_count = patch_starts.shape[0]
    slot_ids = jnp.arange(patch_count, dtype=jnp.int32)
    patch_of = jnp.sum((patch_starts[None, :] <= positions[:, None]).astype(jnp.int32), axis=1) - 1
    matches = (order_starts[:, None] == patch_starts[None, :]).astype(jnp.int32)
    rank_of = jnp.sum(matches * slot_ids[:, None], axis=0)
    one_hot = (patch_of[:, None] == slot_ids[None, :]).astype(jnp.int32)
    return jnp.sum(one_hot * rank_of[None, :], axis=1)


def split_kernel(members, width, where, queries, *rest):
    tensors, outs, sems = rest[:4], rest[4:-1], rest[-1]
    copies = []
    for step in range(members):
        start = pl.multiple_of((where[0] ^ step) * width, width)
        for at, tensor in enumerate(tensors):
            copies.append((tensor.at[:, pl.ds(start, width)], outs[step].at[at]))
        copies.append((queries.at[:, pl.ds(start, width)], outs[members + step]))
    started = [
        pltpu.make_async_copy(src, dst, sems.at[i]) for i, (src, dst) in enumerate(copies)
    ]
    for copy in started:
        copy.start()
    for copy in started:
        copy.wait()


def split_columns(member, members, queries, tensors):
    rows, columns = queries.shape
    width = columns // members
    kinds = len(tensors)
    outs = [jax.ShapeDtypeStruct((kinds, rows, width), queries.dtype)] * members
    outs += [jax.ShapeDtypeStruct((rows, width), queries.dtype)] * members
    anywhere = pl.BlockSpec(memory_space=pl.ANY)
    size = (kinds + 1) * rows * columns * 2
    result = pl.pallas_call(
        functools.partial(split_kernel, members, width),
        out_shape=outs,
        in_specs=[pl.BlockSpec(memory_space=pltpu.SMEM)] + [anywhere] * (kinds + 1),
        out_specs=[anywhere] * len(outs),
        scratch_shapes=[pltpu.SemaphoreType.DMA((members * (kinds + 1),))],
        cost_estimate=pl.CostEstimate(flops=0, bytes_accessed=2 * size, transcendentals=0),
        name="split_columns",
    )(member, queries, *tensors)
    return result[:members], result[members:]


def attend_kernel(sources, blocks, heads, key_rank, query_rank, *refs):
    queries, keys = refs[:sources], refs[sources : sources + blocks]
    outs, stats = refs[sources + blocks : -1], refs[-1]
    head = pl.program_id(0)
    rows = queries[0].shape[0]
    dims = (((1,), (1,)), ((), ()))
    scale = math.log2(math.e) / math.sqrt(HEAD_DIM)
    query = jnp.concatenate([ref[...] for ref in queries], axis=0)
    fresh_keys, fresh_values, stale_keys, stale_values = (
        jnp.concatenate([ref[kind] for ref in keys], axis=0) for kind in range(4)
    )
    fresh_ok = key_rank[...] <= query_rank[...]
    fresh = lax.dot_general(query, fresh_keys, dims, preferred_element_type=jnp.float32)
    stale = lax.dot_general(query, stale_keys, dims, preferred_element_type=jnp.float32)
    scores = jnp.where(fresh_ok, fresh, stale)
    row_max = jnp.max(scores, axis=1, keepdims=True)
    weights = jnp.exp2((scores - row_max) * scale)
    total = jnp.sum(weights, axis=1, keepdims=True)
    fresh_weights = jnp.where(fresh_ok, weights, 0.0).astype(jnp.bfloat16)
    stale_weights = jnp.where(fresh_ok, 0.0, weights).astype(jnp.bfloat16)
    mixed = jnp.dot(fresh_weights, fresh_values, preferred_element_type=jnp.float32)
    mixed = mixed + jnp.dot(stale_weights, stale_values, preferred_element_type=jnp.float32)
    mixed = (mixed / total).astype(jnp.bfloat16)
    at = pl.multiple_of(head * rows, rows)
    for i, out in enumerate(outs):
        out[pl.ds(at, rows), :] = mixed[i * rows : (i + 1) * rows]
    level = row_max * scale + jnp.log2(total)
    high = level.astype(jnp.bfloat16).astype(jnp.float32)
    middle = (level - high).astype(jnp.bfloat16).astype(jnp.float32)
    low = level - high - middle
    lane = lax.broadcasted_iota(jnp.int32, stats.shape, 1) - head * STAT_TERMS
    kept = jnp.where(head == 0, 0.0, stats[...])
    kept = jnp.where(lane == 0, high, kept)
    kept = jnp.where(lane == 1, middle, kept)
    kept = jnp.where(lane == 2, low, kept)
    stats[...] = kept

    @pl.when(head == heads - 1)
    def _():
        turned = kept.T[:STAT_ROWS]
        for i, out in enumerate(outs):
            mine = turned[:, i * rows : (i + 1) * rows].astype(jnp.bfloat16)
            filler = jnp.zeros((STAT_ROWS, HEAD_DIM - rows), jnp.bfloat16)
            out[heads * rows :, :] = jnp.concatenate([mine, filler], axis=1)


def attend(queries, query_rank, keys, key_rank):
    sources, blocks = len(queries), len(keys)
    rows, width = queries[0].shape
    kinds = keys[0].shape[0]
    heads = width // HEAD_DIM
    query_count, key_count = sources * rows, blocks * rows
    whole = lambda *shape: pl.BlockSpec(shape, lambda h: (0,) * len(shape))
    out_rows = heads * rows + STAT_ROWS
    return pl.pallas_call(
        functools.partial(attend_kernel, sources, blocks, heads),
        grid=(heads,),
        out_shape=[jax.ShapeDtypeStruct((out_rows, HEAD_DIM), jnp.bfloat16)] * sources,
        in_specs=[whole(1, key_count), whole(query_count, 1)]
        + [pl.BlockSpec((rows, HEAD_DIM), lambda h: (0, h))] * sources
        + [pl.BlockSpec((kinds, rows, HEAD_DIM), lambda h: (0, 0, h))] * blocks,
        out_specs=[whole(out_rows, HEAD_DIM)] * sources,
        scratch_shapes=[pltpu.VMEM((query_count, HEAD_DIM), jnp.float32)],
        compiler_params=pltpu.CompilerParams(vmem_limit_bytes=VMEM_LIMIT),
        cost_estimate=pl.CostEstimate(
            flops=8 * heads * query_count * key_count * HEAD_DIM,
            bytes_accessed=2 * width * (query_count * 2 + key_count * kinds),
            transcendentals=heads * query_count * key_count,
        ),
        name="attend",
    )(key_rank[None, :], query_rank[:, None], *queries, *keys)


def merge_kernel(parts, members, heads, where, *refs):
    partials, out = refs[:-1], refs[-1]
    rows = out.shape[0]
    for step in range(members):
        group = partials[step * parts : (step + 1) * parts]
        start = (where[0] ^ step) * heads * HEAD_DIM
        levels = []
        for ref in group:
            stats = ref[heads * rows :, :].astype(jnp.float32)
            levels.append(stats.T[:rows])
        for head in range(heads):
            lane = head * STAT_TERMS
            level = [
                one[:, lane : lane + 1] + one[:, lane + 1 : lane + 2] + one[:, lane + 2 : lane + 3]
                for one in levels
            ]
            top = functools.reduce(jnp.maximum, level)
            shares = [jnp.exp2(one - top) for one in level]
            total = functools.reduce(jnp.add, shares)
            mixed = functools.reduce(
                jnp.add,
                [
                    ref[head * rows : (head + 1) * rows, :].astype(jnp.float32) * (share / total)
                    for ref, share in zip(group, shares)
                ],
            )
            at = pl.multiple_of(start + head * HEAD_DIM, HEAD_DIM)
            out[:, pl.ds(at, HEAD_DIM)] = mixed.astype(out.dtype)


def merge(member, partials, rows, heads):
    members, parts = len(partials), len(partials[0])
    flat = [one for group in partials for one in group]
    vmem = pl.BlockSpec(memory_space=pltpu.VMEM)
    return pl.pallas_call(
        functools.partial(merge_kernel, parts, members, heads),
        out_shape=jax.ShapeDtypeStruct((rows, members * heads * HEAD_DIM), jnp.bfloat16),
        in_specs=[pl.BlockSpec(memory_space=pltpu.SMEM)] + [vmem] * len(flat),
        out_specs=vmem,
        compiler_params=pltpu.CompilerParams(vmem_limit_bytes=VMEM_LIMIT),
        name="merge",
    )(member, *flat)


def shards(queries, fresh_keys, fresh_values, stale_keys, stale_values, patch_starts, order_starts):
    devices = lax.axis_size("tok")
    rows = queries.shape[0]
    chips = devices // CORES
    members = min(chips // 2, HEADS)
    groups = chips // members
    heads = HEADS // members
    me = lax.axis_index("tok")
    core, chip = me % CORES, me // CORES
    group, member = chip // members, chip % members
    where = member[None].astype(jnp.int32)

    def hop(array, far, near, side=0):
        flip = (far * members + near) * CORES + side
        if flip == 0:
            return array
        return lax.ppermute(array, "tok", [(i, i ^ flip) for i in range(devices)])

    def positions(far, near, side):
        base = (((group ^ far) * members + (member ^ near)) * CORES + (core ^ side)) * rows
        return base + jnp.arange(rows, dtype=jnp.int32)

    def ranks(places):
        spots = jnp.concatenate([positions(*place) for place in places])
        return token_ranks(spots, patch_starts, order_starts)

    tensors = (fresh_keys, fresh_values, stale_keys, stale_values)
    key_parts, query_parts = split_columns(where, members, queries, tensors)
    order = list(range(members))[::-1]
    keys = {}
    for near in order:
        keys[near, 0] = hop(key_parts[near], 0, near)
    for near in order:
        keys[near, 1] = hop(keys[near, 0], 0, 0, 1)
    places = [(near, side) for near in range(members) for side in range(CORES)]
    key_rank = ranks([(0, near, side) for near, side in places])
    key_blocks = [keys[place] for place in places]
    partials = [[None] * groups for _ in range(members)]
    for far in list(range(groups))[::-1]:
        for first in range(0, members, CHUNK):
            chunk = order[first : first + CHUNK]
            arrived = [hop(query_parts[near], far, near) for near in chunk]
            query_rank = ranks([(far, near, 0) for near in chunk])
            results = attend(arrived, query_rank, key_blocks, key_rank)
            for near, result in zip(chunk, results):
                partials[near][far] = hop(result, far, near)
    return merge(where, partials, rows, heads)


def solution(mesh):
    placed = (P(("groups", "tok"), None),) * 5 + (P("groups"),) * 2
    return jax.shard_map(
        shards, mesh=mesh, in_specs=placed, out_specs=P(("groups", "tok"), None), check_vma=False
    )
```

```python
import functools
import math

import jax
import jax.numpy as jnp
from jax import lax
from jax.experimental import pallas as pl
from jax.experimental.pallas import tpu as pltpu
from jax.sharding import PartitionSpec as P

HEADS = 16
HEAD_DIM = 128
CORES = 2
STAT_ROWS = 16
STAT_TERMS = 4
CHUNK = 4
VMEM_LIMIT = 48 * 1024 * 1024
VMEM_WHOLE = 63 * 1024 * 1024


def token_ranks(positions, patch_starts, order_starts):
    patch_count = patch_starts.shape[0]
    slot_ids = jnp.arange(patch_count, dtype=jnp.int32)
    patch_of = jnp.sum((patch_starts[None, :] <= positions[:, None]).astype(jnp.int32), axis=1) - 1
    matches = (order_starts[:, None] == patch_starts[None, :]).astype(jnp.int32)
    rank_of = jnp.sum(matches * slot_ids[:, None], axis=0)
    one_hot = (patch_of[:, None] == slot_ids[None, :]).astype(jnp.int32)
    return jnp.sum(one_hot * rank_of[None, :], axis=1)


def split_kernel(members, width, where, queries, *rest):
    kinds = 4
    tensors, outs = rest[:kinds], rest[kinds : kinds + 2 * members]
    whole_room, key_room, query_room, into, out_of = rest[kinds + 2 * members :]
    arriving = [
        pltpu.make_async_copy(src, whole_room.at[i], into.at[i])
        for i, src in enumerate((queries,) + tensors)
    ]
    for copy in arriving:
        copy.start()
    steps = list(range(members))[::-1]
    columns = {
        step: pl.ds(pl.multiple_of((where[0] ^ step) * width, width), width) for step in steps
    }
    leaving = []

    def send(room, out):
        leaving.append(pltpu.make_async_copy(room, out, out_of.at[len(leaving)]))
        leaving[-1].start()

    arriving[0].wait()
    for step in steps:
        query_room[step] = whole_room[0, :, columns[step]]
        send(query_room.at[step], outs[members + step])
    for copy in arriving[1:]:
        copy.wait()
    for step in steps:
        for kind in range(kinds):
            key_room[step, kind] = whole_room[1 + kind, :, columns[step]]
        send(key_room.at[step], outs[step])
    for copy in leaving:
        copy.wait()


def split_columns(member, members, queries, tensors):
    rows, columns = queries.shape
    width = columns // members
    kinds = len(tensors)
    outs = [jax.ShapeDtypeStruct((kinds, rows, width), queries.dtype)] * members
    outs += [jax.ShapeDtypeStruct((rows, width), queries.dtype)] * members
    anywhere = pl.BlockSpec(memory_space=pltpu.HBM)
    size = (kinds + 1) * rows * columns * 2
    result = pl.pallas_call(
        functools.partial(split_kernel, members, width),
        out_shape=outs,
        in_specs=[pl.BlockSpec(memory_space=pltpu.SMEM)] + [anywhere] * (kinds + 1),
        out_specs=[anywhere] * len(outs),
        scratch_shapes=[
            pltpu.VMEM((kinds + 1, rows, columns), queries.dtype),
            pltpu.VMEM((members, kinds, rows, width), queries.dtype),
            pltpu.VMEM((members, rows, width), queries.dtype),
            pltpu.SemaphoreType.DMA((kinds + 1,)),
            pltpu.SemaphoreType.DMA((2 * members,)),
        ],
        compiler_params=pltpu.CompilerParams(vmem_limit_bytes=VMEM_WHOLE),
        cost_estimate=pl.CostEstimate(flops=0, bytes_accessed=2 * size, transcendentals=0),
        name="split_columns",
    )(member, queries, *tensors)
    return result[:members], result[members:]


def attend_kernel(sources, blocks, heads, key_rank, query_rank, *refs):
    queries, keys = refs[:sources], refs[sources : sources + blocks]
    outs = refs[sources + blocks :]
    rows = queries[0].shape[0]
    dims = (((1,), (1,)), ((), ()))
    scale = math.log2(math.e) / math.sqrt(HEAD_DIM)
    fresh_ok = key_rank[...] <= query_rank[...]
    lane = lax.broadcasted_iota(jnp.int32, (sources * rows, HEAD_DIM), 1)
    kept = jnp.zeros((sources * rows, HEAD_DIM), jnp.float32)
    for head in range(heads):
        columns = slice(head * HEAD_DIM, (head + 1) * HEAD_DIM)
        query = jnp.concatenate([ref[:, columns] for ref in queries], axis=0)
        fresh_keys, fresh_values, stale_keys, stale_values = (
            jnp.concatenate([ref[kind, :, columns] for ref in keys], axis=0) for kind in range(4)
        )
        fresh = lax.dot_general(query, fresh_keys, dims, preferred_element_type=jnp.float32)
        stale = lax.dot_general(query, stale_keys, dims, preferred_element_type=jnp.float32)
        scores = jnp.where(fresh_ok, fresh, stale)
        row_max = jnp.max(scores, axis=1, keepdims=True)
        weights = jnp.exp2((scores - row_max) * scale)
        total = jnp.sum(weights, axis=1, keepdims=True)
        fresh_weights = jnp.where(fresh_ok, weights, 0.0).astype(jnp.bfloat16)
        stale_weights = jnp.where(fresh_ok, 0.0, weights).astype(jnp.bfloat16)
        mixed = jnp.dot(fresh_weights, fresh_values, preferred_element_type=jnp.float32)
        mixed = mixed + jnp.dot(stale_weights, stale_values, preferred_element_type=jnp.float32)
        mixed = (mixed / total).astype(jnp.bfloat16)
        for i, out in enumerate(outs):
            out[head * rows : (head + 1) * rows, :] = mixed[i * rows : (i + 1) * rows]
        level = row_max * scale + jnp.log2(total)
        high = level.astype(jnp.bfloat16).astype(jnp.float32)
        middle = (level - high).astype(jnp.bfloat16).astype(jnp.float32)
        for term, value in enumerate((high, middle, level - high - middle)):
            kept = jnp.where(lane == head * STAT_TERMS + term, value, kept)
    turned = kept.T[:STAT_ROWS]
    for i, out in enumerate(outs):
        mine = turned[:, i * rows : (i + 1) * rows].astype(jnp.bfloat16)
        filler = jnp.zeros((STAT_ROWS, HEAD_DIM - rows), jnp.bfloat16)
        out[heads * rows :, :] = jnp.concatenate([mine, filler], axis=1)


def attend(queries, query_rank, keys, key_rank):
    sources, blocks = len(queries), len(keys)
    rows, width = queries[0].shape
    kinds = keys[0].shape[0]
    heads = width // HEAD_DIM
    query_count, key_count = sources * rows, blocks * rows
    vmem = pl.BlockSpec(memory_space=pltpu.VMEM)
    out = jax.ShapeDtypeStruct((heads * rows + STAT_ROWS, HEAD_DIM), jnp.bfloat16)
    return pl.pallas_call(
        functools.partial(attend_kernel, sources, blocks, heads),
        out_shape=[out] * sources,
        in_specs=[vmem] * (2 + sources + blocks),
        out_specs=[vmem] * sources,
        compiler_params=pltpu.CompilerParams(vmem_limit_bytes=VMEM_LIMIT),
        cost_estimate=pl.CostEstimate(
            flops=8 * heads * query_count * key_count * HEAD_DIM,
            bytes_accessed=2 * width * (query_count * 2 + key_count * kinds),
            transcendentals=heads * query_count * key_count,
        ),
        name="attend",
    )(key_rank[None, :], query_rank[:, None], *queries, *keys)


def merge_kernel(parts, members, heads, where, *refs):
    partials, out = refs[:-1], refs[-1]
    rows = out.shape[0]
    for step in range(members):
        group = partials[step * parts : (step + 1) * parts]
        start = (where[0] ^ step) * heads * HEAD_DIM
        levels = []
        for ref in group:
            stats = ref[heads * rows :, :].astype(jnp.float32)
            levels.append(stats.T[:rows])
        for head in range(heads):
            lane = head * STAT_TERMS
            level = [
                one[:, lane : lane + 1] + one[:, lane + 1 : lane + 2] + one[:, lane + 2 : lane + 3]
                for one in levels
            ]
            top = functools.reduce(jnp.maximum, level)
            shares = [jnp.exp2(one - top) for one in level]
            total = functools.reduce(jnp.add, shares)
            mixed = functools.reduce(
                jnp.add,
                [
                    ref[head * rows : (head + 1) * rows, :].astype(jnp.float32) * (share / total)
                    for ref, share in zip(group, shares)
                ],
            )
            at = pl.multiple_of(start + head * HEAD_DIM, HEAD_DIM)
            out[:, pl.ds(at, HEAD_DIM)] = mixed.astype(out.dtype)


def merge(member, partials, rows, heads):
    members, parts = len(partials), len(partials[0])
    flat = [one for group in partials for one in group]
    vmem = pl.BlockSpec(memory_space=pltpu.VMEM)
    return pl.pallas_call(
        functools.partial(merge_kernel, parts, members, heads),
        out_shape=jax.ShapeDtypeStruct((rows, members * heads * HEAD_DIM), jnp.bfloat16),
        in_specs=[pl.BlockSpec(memory_space=pltpu.SMEM)] + [vmem] * len(flat),
        out_specs=vmem,
        compiler_params=pltpu.CompilerParams(vmem_limit_bytes=VMEM_LIMIT),
        name="merge",
    )(member, *flat)


def after(array, earlier):
    return lax.optimization_barrier((array, earlier))[0]


def shards(queries, fresh_keys, fresh_values, stale_keys, stale_values, patch_starts, order_starts):
    devices = lax.axis_size("tok")
    rows = queries.shape[0]
    chips = devices // CORES
    members = min(chips // 2, HEADS)
    groups = chips // members
    heads = HEADS // members
    me = lax.axis_index("tok")
    core, chip = me % CORES, me // CORES
    group, member = chip // members, chip % members
    where = member[None].astype(jnp.int32)

    def hop(array, far, near, side=0):
        flip = (far * members + near) * CORES + side
        if flip == 0:
            return array
        return lax.ppermute(array, "tok", [(i, i ^ flip) for i in range(devices)])

    def positions(far, near, side):
        base = (((group ^ far) * members + (member ^ near)) * CORES + (core ^ side)) * rows
        return base + jnp.arange(rows, dtype=jnp.int32)

    def ranks(places):
        spots = jnp.concatenate([positions(*place) for place in places])
        return token_ranks(spots, patch_starts, order_starts)

    tensors = (fresh_keys, fresh_values, stale_keys, stale_values)
    key_parts, query_parts = split_columns(where, members, queries, tensors)
    order = list(range(members))[::-1]
    arrived = {
        (far, near): hop(query_parts[near], far, near)
        for far in range(1, groups)
        for near in order
    }
    first_far = [arrived[1, near] for near in order]
    keys = {}
    for at, near in enumerate(order):
        part = key_parts[near]
        if at > 0:
            part = after(part, first_far[at - 1])
        keys[near, 0] = hop(part, 0, near)
        keys[near, 1] = hop(keys[near, 0], 0, 0, 1)
    for near in order:
        arrived[0, near] = hop(after(query_parts[near], keys[order[1], 0]), 0, near)
    places = [(near, side) for near in range(members) for side in range(CORES)]
    key_rank = ranks([(0, near, side) for near, side in places])
    key_blocks = [keys[place] for place in places]
    partials = [[None] * groups for _ in range(members)]
    for far in list(range(groups))[::-1]:
        for first in range(0, members, CHUNK):
            chunk = order[first : first + CHUNK]
            query_rank = ranks([(far, near, 0) for near in chunk])
            waiting = [arrived[far, near] for near in chunk]
            results = attend(waiting, query_rank, key_blocks, key_rank)
            for near, result in zip(chunk, results):
                partials[near][far] = hop(result, far, near)
    return merge(where, partials, rows, heads)


def solution(mesh):
    placed = (P(("groups", "tok"), None),) * 5 + (P("groups"),) * 2
    return jax.shard_map(
        shards, mesh=mesh, in_specs=placed, out_specs=P(("groups", "tok"), None), check_vma=False
    )
```

```python
import functools
import math

import jax
import jax.numpy as jnp
from jax import lax
from jax.experimental import pallas as pl
from jax.experimental.pallas import tpu as pltpu
from jax.sharding import PartitionSpec as P

HEADS = 16
HEAD_DIM = 128
CORES = 2
STAT_ROWS = 16
STAT_TERMS = 4
CHUNK = 4
VMEM_LIMIT = 48 * 1024 * 1024
VMEM_WHOLE = 63 * 1024 * 1024


def token_ranks(positions, patch_starts, order_starts):
    patch_count = patch_starts.shape[0]
    slot_ids = jnp.arange(patch_count, dtype=jnp.int32)
    patch_of = jnp.sum((patch_starts[None, :] <= positions[:, None]).astype(jnp.int32), axis=1) - 1
    matches = (order_starts[:, None] == patch_starts[None, :]).astype(jnp.int32)
    rank_of = jnp.sum(matches * slot_ids[:, None], axis=0)
    one_hot = (patch_of[:, None] == slot_ids[None, :]).astype(jnp.int32)
    return jnp.sum(one_hot * rank_of[None, :], axis=1)


def split_kernel(members, width, where, queries, *rest):
    kinds = 4
    tensors, outs = rest[:kinds], rest[kinds : kinds + members + 2]
    whole_room, near_room, far_room, into, out_of = rest[kinds + members + 2 :]
    member, core = where[0] // CORES % members, where[0] % CORES
    arriving = [
        pltpu.make_async_copy(src, whole_room.at[i], into.at[i])
        for i, src in enumerate(tensors + (queries,))
    ]
    for copy in arriving[::-1]:
        copy.start()

    def columns(step):
        return pl.ds(pl.multiple_of((member ^ step) * width, width), width)

    leaving = []

    def send(room, out):
        leaving.append(pltpu.make_async_copy(room, out, out_of.at[len(leaving)]))
        leaving[-1].start()

    arriving[kinds].wait()
    for side in range(CORES)[::-1]:
        for pair in range(members // CORES):
            picked = columns(pair * CORES + (core ^ side))
            far_room[side, pair] = whole_room[kinds, :, picked]
        send(far_room.at[side], outs[members + side])
    for copy in arriving[:kinds]:
        copy.wait()
    for step in range(members)[::-1]:
        for kind in range(kinds + 1):
            near_room[step, kind] = whole_room[kind, :, columns(step)]
        send(near_room.at[step], outs[step])
    for copy in leaving:
        copy.wait()


def split_columns(where, members, queries, tensors):
    rows, columns = queries.shape
    width = columns // members
    kinds = len(tensors) + 1
    near = (kinds, rows, width)
    far = (members // CORES, rows, width)
    anywhere = pl.BlockSpec(memory_space=pl.ANY)
    size = kinds * rows * columns * 2
    result = pl.pallas_call(
        functools.partial(split_kernel, members, width),
        out_shape=[jax.ShapeDtypeStruct(near, queries.dtype)] * members
        + [jax.ShapeDtypeStruct(far, queries.dtype)] * CORES,
        in_specs=[pl.BlockSpec(memory_space=pltpu.SMEM)] + [anywhere] * kinds,
        out_specs=[anywhere] * (members + CORES),
        scratch_shapes=[
            pltpu.VMEM((kinds, rows, columns), queries.dtype),
            pltpu.VMEM((members,) + near, queries.dtype),
            pltpu.VMEM((CORES,) + far, queries.dtype),
            pltpu.SemaphoreType.DMA((kinds,)),
            pltpu.SemaphoreType.DMA((members + CORES,)),
        ],
        compiler_params=pltpu.CompilerParams(vmem_limit_bytes=VMEM_WHOLE),
        cost_estimate=pl.CostEstimate(flops=0, bytes_accessed=2 * size, transcendentals=0),
        name="split_columns",
    )(where, queries, *tensors)
    return result[:members], result[members:]


def attend_kernel(picks, arrays, blocks, heads, key_rank, query_rank, *refs):
    queries = [refs[array].at[at] for array, at in picks]
    keys, outs = refs[arrays : arrays + blocks], refs[arrays + blocks :]
    places = [out.at[at] for out in outs for at in range(out.shape[0])]
    rows = queries[0].shape[0]
    dims = (((1,), (1,)), ((), ()))
    scale = math.log2(math.e) / math.sqrt(HEAD_DIM)
    fresh_ok = key_rank[...] <= query_rank[...]
    lane = lax.broadcasted_iota(jnp.int32, (len(picks) * rows, HEAD_DIM), 1)
    kept = jnp.zeros((len(picks) * rows, HEAD_DIM), jnp.float32)
    for head in range(heads):
        columns = slice(head * HEAD_DIM, (head + 1) * HEAD_DIM)
        query = jnp.concatenate([ref[:, columns] for ref in queries], axis=0)
        fresh_keys, fresh_values, stale_keys, stale_values = (
            jnp.concatenate([ref[kind, :, columns] for ref in keys], axis=0) for kind in range(4)
        )
        fresh = lax.dot_general(query, fresh_keys, dims, preferred_element_type=jnp.float32)
        stale = lax.dot_general(query, stale_keys, dims, preferred_element_type=jnp.float32)
        scores = jnp.where(fresh_ok, fresh, stale)
        row_max = jnp.max(scores, axis=1, keepdims=True)
        weights = jnp.exp2((scores - row_max) * scale)
        total = jnp.sum(weights, axis=1, keepdims=True)
        fresh_weights = jnp.where(fresh_ok, weights, 0.0).astype(jnp.bfloat16)
        stale_weights = jnp.where(fresh_ok, 0.0, weights).astype(jnp.bfloat16)
        mixed = jnp.dot(fresh_weights, fresh_values, preferred_element_type=jnp.float32)
        mixed = mixed + jnp.dot(stale_weights, stale_values, preferred_element_type=jnp.float32)
        mixed = (mixed / total).astype(jnp.bfloat16)
        for i, place in enumerate(places):
            place[head * rows : (head + 1) * rows, :] = mixed[i * rows : (i + 1) * rows]
        level = row_max * scale + jnp.log2(total)
        high = level.astype(jnp.bfloat16).astype(jnp.float32)
        middle = (level - high).astype(jnp.bfloat16).astype(jnp.float32)
        for term, value in enumerate((high, middle, level - high - middle)):
            kept = jnp.where(lane == head * STAT_TERMS + term, value, kept)
    turned = kept.T[:STAT_ROWS]
    for i, place in enumerate(places):
        mine = turned[:, i * rows : (i + 1) * rows].astype(jnp.bfloat16)
        filler = jnp.zeros((STAT_ROWS, HEAD_DIM - rows), jnp.bfloat16)
        place[heads * rows :, :] = jnp.concatenate([mine, filler], axis=1)


def attend(arrays, picks, per_out, query_rank, keys, key_rank):
    blocks = len(keys)
    kinds, rows, width = keys[0].shape
    heads = width // HEAD_DIM
    query_count, key_count = len(picks) * rows, blocks * rows
    vmem = pl.BlockSpec(memory_space=pltpu.VMEM)
    out = jax.ShapeDtypeStruct((per_out, heads * rows + STAT_ROWS, HEAD_DIM), jnp.bfloat16)
    outs = len(picks) // per_out
    return pl.pallas_call(
        functools.partial(attend_kernel, picks, len(arrays), blocks, heads),
        out_shape=[out] * outs,
        in_specs=[vmem] * (2 + len(arrays) + blocks),
        out_specs=[vmem] * outs,
        compiler_params=pltpu.CompilerParams(vmem_limit_bytes=VMEM_LIMIT),
        cost_estimate=pl.CostEstimate(
            flops=8 * heads * query_count * key_count * HEAD_DIM,
            bytes_accessed=2 * width * (query_count * 2 + key_count * kinds),
            transcendentals=heads * query_count * key_count,
        ),
        name="attend",
    )(key_rank[None, :], query_rank[:, None], *arrays, *keys)


def merge_kernel(parts, members, heads, where, *refs):
    out = refs[-1]
    rows = out.shape[0]
    near, far = refs[:members], refs[members:-1]
    member, core = where[0] // CORES % members, where[0] % CORES
    for step in range(members):
        pair, side = step // CORES, step % CORES
        group = [near[pair * CORES].at[0][...]]
        for other in range(1, CORES):
            wanted = (core ^ side) == other
            group[0] = jnp.where(wanted, near[pair * CORES + other].at[0][...], group[0])
        for part in range(parts - 1):
            group.append(far[(part * (members // CORES) + pair) * CORES + side].at[0][...])
        start = (member ^ (pair * CORES + (core ^ side))) * heads * HEAD_DIM
        levels = [one[heads * rows :].astype(jnp.float32).T[:rows] for one in group]
        for head in range(heads):
            lane = head * STAT_TERMS
            level = [
                one[:, lane : lane + 1] + one[:, lane + 1 : lane + 2] + one[:, lane + 2 : lane + 3]
                for one in levels
            ]
            top = functools.reduce(jnp.maximum, level)
            shares = [jnp.exp2(one - top) for one in level]
            total = functools.reduce(jnp.add, shares)
            mixed = functools.reduce(
                jnp.add,
                [
                    one[head * rows : (head + 1) * rows].astype(jnp.float32) * (share / total)
                    for one, share in zip(group, shares)
                ],
            )
            at = pl.multiple_of(start + head * HEAD_DIM, HEAD_DIM)
            out[:, pl.ds(at, HEAD_DIM)] = mixed.astype(out.dtype)


def merge(where, near, far, rows, heads):
    members = len(near)
    pairs = members // CORES
    parts = 1 + len(far) // (pairs * CORES)
    vmem = pl.BlockSpec(memory_space=pltpu.VMEM)
    return pl.pallas_call(
        functools.partial(merge_kernel, parts, members, heads),
        out_shape=jax.ShapeDtypeStruct((rows, members * heads * HEAD_DIM), jnp.bfloat16),
        in_specs=[pl.BlockSpec(memory_space=pltpu.SMEM)] + [vmem] * (len(near) + len(far)),
        out_specs=vmem,
        compiler_params=pltpu.CompilerParams(vmem_limit_bytes=VMEM_LIMIT),
        name="merge",
    )(where, *near, *far)


def after(array, earlier):
    return lax.optimization_barrier((array, earlier))[0]


def shards(queries, fresh_keys, fresh_values, stale_keys, stale_values, patch_starts, order_starts):
    devices = lax.axis_size("tok")
    rows = queries.shape[0]
    chips = devices // CORES
    members = min(chips // 2, HEADS)
    groups = chips // members
    heads = HEADS // members
    me = lax.axis_index("tok")
    core, chip = me % CORES, me // CORES
    group, member = chip // members, chip % members
    where = me[None].astype(jnp.int32)
    pairs = members // CORES

    def hop(array, far, near, side=0):
        flip = (far * members + near) * CORES + side
        if flip == 0:
            return array
        return lax.ppermute(array, "tok", [(i, i ^ flip) for i in range(devices)])

    def far_hop(array, far, pair):
        flips = [(far * members + pair * CORES + i % CORES) * CORES for i in range(devices)]
        return lax.ppermute(array, "tok", [(i, i ^ flips[i]) for i in range(devices)])

    def ranks(places):
        spots = [
            (((group ^ far) * members + (member ^ near)) * CORES + (core ^ side)) * rows
            + jnp.arange(rows, dtype=jnp.int32)
            for far, near, side in places
        ]
        return token_ranks(jnp.concatenate(spots), patch_starts, order_starts)

    tensors = (fresh_keys, fresh_values, stale_keys, stale_values)
    blocks, (mine, others) = split_columns(where, members, queries, tensors)
    order = list(range(members))[::-1]
    other_mine = hop(others, 0, 0, 1)
    arrived = {
        (far, pair): far_hop(jnp.stack([mine[pair], other_mine[pair]]), far, pair)
        for far in range(1, groups)
        for pair in range(pairs)[::-1]
    }
    keys = {}
    keys[0, 0] = blocks[0]
    keys[0, 1] = hop(after(blocks[0], other_mine), 0, 0, 1)
    for near in order[:-1]:
        keys[near, 0] = hop(blocks[near], 0, near)
        block = keys[near, 0]
        for pair in range(pairs):
            block = after(block, arrived[1, pair])
        keys[near, 1] = hop(block, 0, 0, 1)
    key_rank = ranks([(0, near, side) for near in range(members) for side in range(CORES)])
    key_blocks = [keys[near, side] for near in range(members) for side in range(CORES)]
    far_parts, near_parts = [], [None] * members
    for far in range(1, groups):
        for first in range(0, pairs, CHUNK // CORES):
            chunk = list(range(first, min(pairs, first + CHUNK // CORES)))
            query_rank = ranks(
                [(far, pair * CORES + core, side) for pair in chunk for side in range(CORES)]
            )
            waiting = [arrived[far, pair] for pair in chunk]
            picks = [(at, side) for at in range(len(chunk)) for side in range(CORES)]
            results = attend(waiting, picks, CORES, query_rank, key_blocks, key_rank)
            for pair, result in zip(chunk, results):
                back = far_hop(result, far, pair)
                far_parts += [back[:1], hop(back[1:], 0, 0, 1)]
    for first in range(0, members, CHUNK):
        chunk = list(range(first, min(members, first + CHUNK)))
        query_rank = ranks([(0, near, 0) for near in chunk])
        waiting = [keys[near, 0] for near in chunk]
        picks = [(at, len(tensors)) for at in range(len(chunk))]
        results = attend(waiting, picks, 1, query_rank, key_blocks, key_rank)
        for near, result in zip(chunk, results):
            near_parts[near] = hop(result, 0, near)
    return merge(where, near_parts, far_parts, rows, heads)


def solution(mesh):
    placed = (P(("groups", "tok"), None),) * 5 + (P("groups"),) * 2
    return jax.shard_map(
        shards, mesh=mesh, in_specs=placed, out_specs=P(("groups", "tok"), None), check_vma=False
    )
```

```python
import functools
import math

import jax
import jax.numpy as jnp
from jax import lax
from jax.experimental import pallas as pl
from jax.experimental.pallas import tpu as pltpu
from jax.sharding import PartitionSpec as P

HEADS = 16
HEAD_DIM = 128
CORES = 2
STAT_ROWS = 16
STAT_TERMS = 4
CHUNK = 4
VMEM_LIMIT = 48 * 1024 * 1024
VMEM_WHOLE = 63 * 1024 * 1024


def token_ranks(positions, patch_starts, order_starts):
    patch_count = patch_starts.shape[0]
    slot_ids = jnp.arange(patch_count, dtype=jnp.int32)
    patch_of = jnp.sum((patch_starts[None, :] <= positions[:, None]).astype(jnp.int32), axis=1) - 1
    matches = (order_starts[:, None] == patch_starts[None, :]).astype(jnp.int32)
    rank_of = jnp.sum(matches * slot_ids[:, None], axis=0)
    one_hot = (patch_of[:, None] == slot_ids[None, :]).astype(jnp.int32)
    return jnp.sum(one_hot * rank_of[None, :], axis=1)


def split_kernel(members, width, where, queries, *rest):
    kinds = 4
    tensors, outs = rest[:kinds], rest[kinds : kinds + members + 2]
    whole_room, near_room, far_room, into, out_of = rest[kinds + members + 2 :]
    member, core = where[0] // CORES % members, where[0] % CORES
    arriving = [
        pltpu.make_async_copy(src, whole_room.at[i], into.at[i])
        for i, src in enumerate(tensors + (queries,))
    ]
    for copy in arriving[::-1]:
        copy.start()

    def columns(step):
        return pl.ds(pl.multiple_of((member ^ step) * width, width), width)

    leaving = []

    def send(room, out):
        leaving.append(pltpu.make_async_copy(room, out, out_of.at[len(leaving)]))
        leaving[-1].start()

    arriving[kinds].wait()
    for side in range(CORES)[::-1]:
        for pair in range(members // CORES):
            picked = columns(pair * CORES + (core ^ side))
            far_room[side, pair] = whole_room[kinds, :, picked]
        send(far_room.at[side], outs[members + side])
    for copy in arriving[:kinds]:
        copy.wait()
    for step in range(members)[::-1]:
        for kind in range(kinds + 1):
            near_room[step, kind] = whole_room[kind, :, columns(step)]
        send(near_room.at[step], outs[step])
    for copy in leaving:
        copy.wait()


def split_columns(where, members, queries, tensors):
    rows, columns = queries.shape
    width = columns // members
    kinds = len(tensors) + 1
    near = (kinds, rows, width)
    far = (members // CORES, rows, width)
    anywhere = pl.BlockSpec(memory_space=pl.ANY)
    size = kinds * rows * columns * 2
    result = pl.pallas_call(
        functools.partial(split_kernel, members, width),
        out_shape=[jax.ShapeDtypeStruct(near, queries.dtype)] * members
        + [jax.ShapeDtypeStruct(far, queries.dtype)] * CORES,
        in_specs=[pl.BlockSpec(memory_space=pltpu.SMEM)] + [anywhere] * kinds,
        out_specs=[anywhere] * (members + CORES),
        scratch_shapes=[
            pltpu.VMEM((kinds, rows, columns), queries.dtype),
            pltpu.VMEM((members,) + near, queries.dtype),
            pltpu.VMEM((CORES,) + far, queries.dtype),
            pltpu.SemaphoreType.DMA((kinds,)),
            pltpu.SemaphoreType.DMA((members + CORES,)),
        ],
        compiler_params=pltpu.CompilerParams(vmem_limit_bytes=VMEM_WHOLE),
        cost_estimate=pl.CostEstimate(flops=0, bytes_accessed=2 * size, transcendentals=0),
        name="split_columns",
    )(where, queries, *tensors)
    return result[:members], result[members:]


def attend_kernel(picks, arrays, blocks, heads, key_rank, query_rank, *refs):
    queries = [refs[array].at[at] for array, at in picks]
    keys, outs = refs[arrays : arrays + blocks], refs[arrays + blocks :]
    places = [out.at[at] for out in outs for at in range(out.shape[0])]
    rows = queries[0].shape[0]
    dims = (((1,), (1,)), ((), ()))
    scale = math.log2(math.e) / math.sqrt(HEAD_DIM)
    fresh_ok = key_rank[...] <= query_rank[...]
    lane = lax.broadcasted_iota(jnp.int32, (len(picks) * rows, HEAD_DIM), 1)
    kept = jnp.zeros((len(picks) * rows, HEAD_DIM), jnp.float32)
    for head in range(heads):
        columns = slice(head * HEAD_DIM, (head + 1) * HEAD_DIM)
        query = jnp.concatenate([ref[:, columns] for ref in queries], axis=0)
        fresh_keys, fresh_values, stale_keys, stale_values = (
            jnp.concatenate([ref[kind, :, columns] for ref in keys], axis=0) for kind in range(4)
        )
        fresh = lax.dot_general(query, fresh_keys, dims, preferred_element_type=jnp.float32)
        stale = lax.dot_general(query, stale_keys, dims, preferred_element_type=jnp.float32)
        scores = jnp.where(fresh_ok, fresh, stale)
        row_max = jnp.max(scores, axis=1, keepdims=True)
        weights = jnp.exp2((scores - row_max) * scale)
        total = jnp.sum(weights, axis=1, keepdims=True)
        fresh_weights = jnp.where(fresh_ok, weights, 0.0).astype(jnp.bfloat16)
        stale_weights = jnp.where(fresh_ok, 0.0, weights).astype(jnp.bfloat16)
        mixed = jnp.dot(fresh_weights, fresh_values, preferred_element_type=jnp.float32)
        mixed = mixed + jnp.dot(stale_weights, stale_values, preferred_element_type=jnp.float32)
        mixed = (mixed / total).astype(jnp.bfloat16)
        for i, place in enumerate(places):
            place[head * rows : (head + 1) * rows, :] = mixed[i * rows : (i + 1) * rows]
        level = row_max * scale + jnp.log2(total)
        high = level.astype(jnp.bfloat16).astype(jnp.float32)
        middle = (level - high).astype(jnp.bfloat16).astype(jnp.float32)
        for term, value in enumerate((high, middle, level - high - middle)):
            kept = jnp.where(lane == head * STAT_TERMS + term, value, kept)
    turned = kept.T[:STAT_ROWS]
    for i, place in enumerate(places):
        mine = turned[:, i * rows : (i + 1) * rows].astype(jnp.bfloat16)
        filler = jnp.zeros((STAT_ROWS, HEAD_DIM - rows), jnp.bfloat16)
        place[heads * rows :, :] = jnp.concatenate([mine, filler], axis=1)


def attend(arrays, picks, per_out, query_rank, keys, key_rank):
    blocks = len(keys)
    kinds, rows, width = keys[0].shape
    heads = width // HEAD_DIM
    query_count, key_count = len(picks) * rows, blocks * rows
    vmem = pl.BlockSpec(memory_space=pltpu.VMEM)
    out = jax.ShapeDtypeStruct((per_out, heads * rows + STAT_ROWS, HEAD_DIM), jnp.bfloat16)
    outs = len(picks) // per_out
    return pl.pallas_call(
        functools.partial(attend_kernel, picks, len(arrays), blocks, heads),
        out_shape=[out] * outs,
        in_specs=[vmem] * (2 + len(arrays) + blocks),
        out_specs=[vmem] * outs,
        compiler_params=pltpu.CompilerParams(vmem_limit_bytes=VMEM_LIMIT),
        cost_estimate=pl.CostEstimate(
            flops=8 * heads * query_count * key_count * HEAD_DIM,
            bytes_accessed=2 * width * (query_count * 2 + key_count * kinds),
            transcendentals=heads * query_count * key_count,
        ),
        name="attend",
    )(key_rank[None, :], query_rank[:, None], *arrays, *keys)


def merge_kernel(parts, members, heads, where, *refs):
    out = refs[-1]
    rows = out.shape[0]
    near, far = refs[:members], refs[members:-1]
    member, core = where[0] // CORES % members, where[0] % CORES
    for step in range(members):
        pair, side = step // CORES, step % CORES
        group = [near[pair * CORES].at[0][...]]
        for other in range(1, CORES):
            wanted = (core ^ side) == other
            group[0] = jnp.where(wanted, near[pair * CORES + other].at[0][...], group[0])
        for part in range(parts - 1):
            group.append(far[(part * (members // CORES) + pair) * CORES + side].at[0][...])
        start = (member ^ (pair * CORES + (core ^ side))) * heads * HEAD_DIM
        levels = [one[heads * rows :].astype(jnp.float32).T[:rows] for one in group]
        for head in range(heads):
            lane = head * STAT_TERMS
            level = [
                one[:, lane : lane + 1] + one[:, lane + 1 : lane + 2] + one[:, lane + 2 : lane + 3]
                for one in levels
            ]
            top = functools.reduce(jnp.maximum, level)
            shares = [jnp.exp2(one - top) for one in level]
            total = functools.reduce(jnp.add, shares)
            mixed = functools.reduce(
                jnp.add,
                [
                    one[head * rows : (head + 1) * rows].astype(jnp.float32) * (share / total)
                    for one, share in zip(group, shares)
                ],
            )
            at = pl.multiple_of(start + head * HEAD_DIM, HEAD_DIM)
            out[:, pl.ds(at, HEAD_DIM)] = mixed.astype(out.dtype)


def merge(where, near, far, rows, heads):
    members = len(near)
    pairs = members // CORES
    parts = 1 + len(far) // (pairs * CORES)
    vmem = pl.BlockSpec(memory_space=pltpu.VMEM)
    return pl.pallas_call(
        functools.partial(merge_kernel, parts, members, heads),
        out_shape=jax.ShapeDtypeStruct((rows, members * heads * HEAD_DIM), jnp.bfloat16),
        in_specs=[pl.BlockSpec(memory_space=pltpu.SMEM)] + [vmem] * (len(near) + len(far)),
        out_specs=vmem,
        compiler_params=pltpu.CompilerParams(vmem_limit_bytes=VMEM_LIMIT),
        name="merge",
    )(where, *near, *far)


def after(array, earlier):
    return lax.optimization_barrier((array, earlier))[0]


def shards(queries, fresh_keys, fresh_values, stale_keys, stale_values, patch_starts, order_starts):
    devices = lax.axis_size("tok")
    rows = queries.shape[0]
    chips = devices // CORES
    members = min(chips // 2, HEADS)
    groups = chips // members
    heads = HEADS // members
    me = lax.axis_index("tok")
    core, chip = me % CORES, me // CORES
    group, member = chip // members, chip % members
    where = me[None].astype(jnp.int32)
    pairs = members // CORES

    def hop(array, far, near, side=0):
        flip = (far * members + near) * CORES + side
        if flip == 0:
            return array
        return lax.ppermute(array, "tok", [(i, i ^ flip) for i in range(devices)])

    def far_hop(array, far, pair):
        flips = [(far * members + pair * CORES + i % CORES) * CORES for i in range(devices)]
        return lax.ppermute(array, "tok", [(i, i ^ flips[i]) for i in range(devices)])

    def ranks(places):
        spots = [
            (((group ^ far) * members + (member ^ near)) * CORES + (core ^ side)) * rows
            + jnp.arange(rows, dtype=jnp.int32)
            for far, near, side in places
        ]
        return token_ranks(jnp.concatenate(spots), starts_later, order_starts)

    tensors = (fresh_keys, fresh_values, stale_keys, stale_values)
    blocks, (mine, others) = split_columns(where, members, queries, tensors)
    order = list(range(members))[::-1]
    other_mine = hop(others, 0, 0, 1)
    arrived = {
        (far, pair): far_hop(jnp.stack([mine[pair], other_mine[pair]]), far, pair)
        for far in range(1, groups)
        for pair in range(pairs)[::-1]
    }
    keys = {}
    keys[0, 0] = blocks[0]
    keys[0, 1] = hop(after(blocks[0], other_mine), 0, 0, 1)
    for near in order[:-1]:
        keys[near, 0] = hop(blocks[near], 0, near)
        block = keys[near, 0]
        block = after(block, arrived[1, 0])
        keys[near, 1] = hop(block, 0, 0, 1)
    starts_later = after(patch_starts, keys[order[0], 0])
    key_rank = ranks([(0, near, side) for near in range(members) for side in range(CORES)])
    key_blocks = [keys[near, side] for near in range(members) for side in range(CORES)]
    far_parts, near_parts = [], [None] * members
    for far in range(1, groups):
        for first in range(0, pairs, CHUNK // CORES):
            chunk = list(range(first, min(pairs, first + CHUNK // CORES)))
            query_rank = ranks(
                [(far, pair * CORES + core, side) for pair in chunk for side in range(CORES)]
            )
            waiting = [arrived[far, pair] for pair in chunk]
            picks = [(at, side) for at in range(len(chunk)) for side in range(CORES)]
            results = attend(waiting, picks, CORES, query_rank, key_blocks, key_rank)
            for pair, result in zip(chunk, results):
                back = far_hop(result, far, pair)
                far_parts += [back[:1], hop(back[1:], 0, 0, 1)]
    for first in range(0, members, CHUNK):
        chunk = list(range(first, min(members, first + CHUNK)))
        query_rank = ranks([(0, near, 0) for near in chunk])
        waiting = [keys[near, 0] for near in chunk]
        picks = [(at, len(tensors)) for at in range(len(chunk))]
        results = attend(waiting, picks, 1, query_rank, key_blocks, key_rank)
        for near, result in zip(chunk, results):
            near_parts[near] = hop(result, 0, near)
    return merge(where, near_parts, far_parts, rows, heads)


def solution(mesh):
    placed = (P(("groups", "tok"), None),) * 5 + (P("groups"),) * 2
    return jax.shard_map(
        shards, mesh=mesh, in_specs=placed, out_specs=P(("groups", "tok"), None), check_vma=False
    )
```

```python
import functools
import math

import jax
import jax.numpy as jnp
from jax import lax
from jax.experimental import pallas as pl
from jax.experimental.pallas import tpu as pltpu
from jax.sharding import PartitionSpec as P

HEADS = 16
HEAD_DIM = 128
CORES = 2
STAT_ROWS = 16
STAT_TERMS = 4
CHUNK = 4
VMEM_LIMIT = 48 * 1024 * 1024
VMEM_WHOLE = 63 * 1024 * 1024


def token_ranks(positions, patch_starts, order_starts):
    patch_count = patch_starts.shape[0]
    slot_ids = jnp.arange(patch_count, dtype=jnp.int32)
    patch_of = jnp.sum((patch_starts[None, :] <= positions[:, None]).astype(jnp.int32), axis=1) - 1
    matches = (order_starts[:, None] == patch_starts[None, :]).astype(jnp.int32)
    rank_of = jnp.sum(matches * slot_ids[:, None], axis=0)
    one_hot = (patch_of[:, None] == slot_ids[None, :]).astype(jnp.int32)
    return jnp.sum(one_hot * rank_of[None, :], axis=1)


def split_kernel(members, width, where, queries, *rest):
    kinds = 4
    tensors, outs = rest[:kinds], rest[kinds : kinds + members + 2]
    whole_room, near_room, far_room, into, out_of = rest[kinds + members + 2 :]
    member, core = where[0] // CORES % members, where[0] % CORES
    arriving = [
        pltpu.make_async_copy(src, whole_room.at[i], into.at[i])
        for i, src in enumerate(tensors + (queries,))
    ]
    for copy in arriving[::-1]:
        copy.start()

    def columns(step):
        return pl.ds(pl.multiple_of((member ^ step) * width, width), width)

    leaving = []

    def send(room, out):
        leaving.append(pltpu.make_async_copy(room, out, out_of.at[len(leaving)]))
        leaving[-1].start()

    arriving[kinds].wait()
    for side in range(CORES)[::-1]:
        for pair in range(members // CORES):
            picked = columns(pair * CORES + (core ^ side))
            far_room[side, pair] = whole_room[kinds, :, picked]
        send(far_room.at[side], outs[members + side])
    for copy in arriving[:kinds]:
        copy.wait()
    for step in range(members)[::-1]:
        depth = outs[step].shape[0]
        for kind in range(depth):
            near_room[step, kind] = whole_room[kind, :, columns(step)]
        send(near_room.at[step, pl.ds(0, depth)], outs[step])
    for copy in leaving:
        copy.wait()


def split_columns(where, members, queries, tensors):
    rows, columns = queries.shape
    width = columns // members
    kinds = len(tensors) + 1
    near = (kinds, rows, width)
    far = (members // CORES, rows, width)
    anywhere = pl.BlockSpec(memory_space=pl.ANY)
    size = kinds * rows * columns * 2
    result = pl.pallas_call(
        functools.partial(split_kernel, members, width),
        out_shape=[jax.ShapeDtypeStruct(near, queries.dtype)] * CORES
        + [jax.ShapeDtypeStruct((kinds - 1,) + near[1:], queries.dtype)] * (members - CORES)
        + [jax.ShapeDtypeStruct(far, queries.dtype)] * CORES,
        in_specs=[pl.BlockSpec(memory_space=pltpu.SMEM)] + [anywhere] * kinds,
        out_specs=[anywhere] * (members + CORES),
        scratch_shapes=[
            pltpu.VMEM((kinds, rows, columns), queries.dtype),
            pltpu.VMEM((members,) + near, queries.dtype),
            pltpu.VMEM((CORES,) + far, queries.dtype),
            pltpu.SemaphoreType.DMA((kinds,)),
            pltpu.SemaphoreType.DMA((members + CORES,)),
        ],
        compiler_params=pltpu.CompilerParams(vmem_limit_bytes=VMEM_WHOLE),
        cost_estimate=pl.CostEstimate(flops=0, bytes_accessed=2 * size, transcendentals=0),
        name="split_columns",
    )(where, queries, *tensors)
    return result[:members], result[members:]


def attend_kernel(picks, arrays, blocks, heads, key_rank, query_rank, *refs):
    queries = [refs[array].at[at] for array, at in picks]
    keys, outs = refs[arrays : arrays + blocks], refs[arrays + blocks :]
    places = [out.at[at] for out in outs for at in range(out.shape[0])]
    rows = queries[0].shape[0]
    dims = (((1,), (1,)), ((), ()))
    scale = math.log2(math.e) / math.sqrt(HEAD_DIM)
    fresh_ok = key_rank[...] <= query_rank[...]
    lane = lax.broadcasted_iota(jnp.int32, (len(picks) * rows, HEAD_DIM), 1)
    kept = jnp.zeros((len(picks) * rows, HEAD_DIM), jnp.float32)
    for head in range(heads):
        columns = slice(head * HEAD_DIM, (head + 1) * HEAD_DIM)
        query = jnp.concatenate([ref[:, columns] for ref in queries], axis=0)
        fresh_keys, fresh_values, stale_keys, stale_values = (
            jnp.concatenate([ref[kind, :, columns] for ref in keys], axis=0) for kind in range(4)
        )
        fresh = lax.dot_general(query, fresh_keys, dims, preferred_element_type=jnp.float32)
        stale = lax.dot_general(query, stale_keys, dims, preferred_element_type=jnp.float32)
        scores = jnp.where(fresh_ok, fresh, stale)
        row_max = jnp.max(scores, axis=1, keepdims=True)
        weights = jnp.exp2((scores - row_max) * scale)
        total = jnp.sum(weights, axis=1, keepdims=True)
        fresh_weights = jnp.where(fresh_ok, weights, 0.0).astype(jnp.bfloat16)
        stale_weights = jnp.where(fresh_ok, 0.0, weights).astype(jnp.bfloat16)
        mixed = jnp.dot(fresh_weights, fresh_values, preferred_element_type=jnp.float32)
        mixed = mixed + jnp.dot(stale_weights, stale_values, preferred_element_type=jnp.float32)
        mixed = (mixed / total).astype(jnp.bfloat16)
        for i, place in enumerate(places):
            place[head * rows : (head + 1) * rows, :] = mixed[i * rows : (i + 1) * rows]
        level = row_max * scale + jnp.log2(total)
        high = level.astype(jnp.bfloat16).astype(jnp.float32)
        middle = (level - high).astype(jnp.bfloat16).astype(jnp.float32)
        for term, value in enumerate((high, middle, level - high - middle)):
            kept = jnp.where(lane == head * STAT_TERMS + term, value, kept)
    turned = kept.T[:STAT_ROWS]
    for i, place in enumerate(places):
        mine = turned[:, i * rows : (i + 1) * rows].astype(jnp.bfloat16)
        filler = jnp.zeros((STAT_ROWS, HEAD_DIM - rows), jnp.bfloat16)
        place[heads * rows :, :] = jnp.concatenate([mine, filler], axis=1)


def attend(arrays, picks, depths, query_rank, keys, key_rank):
    blocks = len(keys)
    rows, width = keys[0].shape[1:]
    heads = width // HEAD_DIM
    query_count, key_count = len(picks) * rows, blocks * rows
    vmem = pl.BlockSpec(memory_space=pltpu.VMEM)
    tile = (heads * rows + STAT_ROWS, HEAD_DIM)
    return pl.pallas_call(
        functools.partial(attend_kernel, picks, len(arrays), blocks, heads),
        out_shape=[jax.ShapeDtypeStruct((depth,) + tile, jnp.bfloat16) for depth in depths],
        in_specs=[vmem] * (2 + len(arrays) + blocks),
        out_specs=[vmem] * len(depths),
        compiler_params=pltpu.CompilerParams(vmem_limit_bytes=VMEM_LIMIT),
        cost_estimate=pl.CostEstimate(
            flops=8 * heads * query_count * key_count * HEAD_DIM,
            bytes_accessed=2 * width * (query_count * 2 + key_count * 4),
            transcendentals=heads * query_count * key_count,
        ),
        name="attend",
    )(key_rank[None, :], query_rank[:, None], *arrays, *keys)


def merge_kernel(chosen, parts, members, heads, where, *refs):
    out, room, sems = refs[-3:]
    rows = out.shape[0]
    width = heads * HEAD_DIM
    member, core = where[0] // CORES % members, where[0] % CORES
    refs = list(refs)
    leaving = []
    for place, pair in enumerate(chosen):
        direct = [refs.pop(0) for _ in range(CORES)] if pair == 0 else None
        crossed = [refs.pop(0) for _ in range((parts if pair else parts - 1) * CORES)]
        for side in range(CORES):
            group = [one.at[0][...] for one in crossed[side::CORES]]
            if pair == 0:
                one = direct[0].at[0][...]
                for step in range(1, CORES):
                    one = jnp.where((core ^ side) == step, direct[step].at[0][...], one)
                group.append(one)
            at = place * CORES + side
            levels = [one[heads * rows :].astype(jnp.float32).T[:rows] for one in group]
            for head in range(heads):
                lane = head * STAT_TERMS
                level = [
                    one[:, lane : lane + 1]
                    + one[:, lane + 1 : lane + 2]
                    + one[:, lane + 2 : lane + 3]
                    for one in levels
                ]
                top = functools.reduce(jnp.maximum, level)
                shares = [jnp.exp2(one - top) for one in level]
                total = functools.reduce(jnp.add, shares)
                mixed = functools.reduce(
                    jnp.add,
                    [
                        one[head * rows : (head + 1) * rows].astype(jnp.float32) * (share / total)
                        for one, share in zip(group, shares)
                    ],
                )
                room[at, :, head * HEAD_DIM : (head + 1) * HEAD_DIM] = mixed.astype(out.dtype)
            start = pl.multiple_of((member ^ (pair * CORES + (core ^ side))) * width, width)
            columns = out.at[:, pl.ds(start, width)]
            leaving.append(pltpu.make_async_copy(room.at[at], columns, sems.at[at]))
            leaving[-1].start()
    for copy in leaving:
        copy.wait()


def merge(where, partials, chosen, parts, members, rows, heads, earlier=None):
    vmem, anywhere = pl.BlockSpec(memory_space=pltpu.VMEM), pl.BlockSpec(memory_space=pl.ANY)
    blocks = len(chosen) * CORES
    operands = [where] + partials + ([] if earlier is None else [earlier])
    specs = [pl.BlockSpec(memory_space=pltpu.SMEM)] + [vmem] * len(partials)
    return pl.pallas_call(
        functools.partial(merge_kernel, chosen, parts, members, heads),
        out_shape=jax.ShapeDtypeStruct((rows, members * heads * HEAD_DIM), jnp.bfloat16),
        in_specs=specs + ([] if earlier is None else [anywhere]),
        out_specs=anywhere,
        scratch_shapes=[
            pltpu.VMEM((blocks, rows, heads * HEAD_DIM), jnp.bfloat16),
            pltpu.SemaphoreType.DMA((blocks,)),
        ],
        input_output_aliases={} if earlier is None else {len(operands) - 1: 0},
        compiler_params=pltpu.CompilerParams(vmem_limit_bytes=VMEM_LIMIT),
        name="merge",
    )(*operands)


def after(array, earlier):
    return lax.optimization_barrier((array, earlier))[0]


def shards(queries, fresh_keys, fresh_values, stale_keys, stale_values, patch_starts, order_starts):
    devices = lax.axis_size("tok")
    rows = queries.shape[0]
    chips = devices // CORES
    members = min(chips // 2, HEADS)
    groups = chips // members
    heads = HEADS // members
    me = lax.axis_index("tok")
    core, chip = me % CORES, me // CORES
    group, member = chip // members, chip % members
    where = me[None].astype(jnp.int32)
    pairs = members // CORES

    def hop(array, far, near, side=0):
        flip = (far * members + near) * CORES + side
        if flip == 0:
            return array
        return lax.ppermute(array, "tok", [(i, i ^ flip) for i in range(devices)])

    def far_hop(array, far, pair):
        flips = [(far * members + pair * CORES + i % CORES) * CORES for i in range(devices)]
        return lax.ppermute(array, "tok", [(i, i ^ flips[i]) for i in range(devices)])

    def ranks(places):
        spots = [
            (((group ^ far) * members + (member ^ near)) * CORES + (core ^ side)) * rows
            + jnp.arange(rows, dtype=jnp.int32)
            for far, near, side in places
        ]
        return token_ranks(jnp.concatenate(spots), starts_later, order_starts)

    tensors = (fresh_keys, fresh_values, stale_keys, stale_values)
    blocks, (mine, others) = split_columns(where, members, queries, tensors)
    order = list(range(members))[::-1]
    other_mine = hop(others, 0, 0, 1)
    payload = [jnp.stack([mine[pair], other_mine[pair]]) for pair in range(pairs)]
    arrived = {
        (far, pair): far_hop(payload[pair], far, pair)
        for far in range(1, groups)
        for pair in range(pairs)[::-1]
    }
    first_far = arrived[1, 0]
    for pair in range(1, pairs):
        arrived[0, pair] = far_hop(after(payload[pair], first_far), 0, pair)
    keys = {}
    keys[0, 0] = blocks[0]
    keys[0, 1] = hop(after(blocks[0], other_mine), 0, 0, 1)
    for near in order[:-1]:
        keys[near, 0] = hop(blocks[near], 0, near)
        keys[near, 1] = hop(after(after(keys[near, 0], first_far), keys[0, 1]), 0, 0, 1)
    starts_later = after(patch_starts, keys[order[0], 0])
    key_rank = ranks([(0, near, side) for near in range(members) for side in range(CORES)])
    key_blocks = [keys[near, side] for near in range(members) for side in range(CORES)]

    def crossing(far, chunk):
        places = [(far, pair * CORES + core, side) for pair in chunk for side in range(CORES)]
        picks = [(at, side) for at in range(len(chunk)) for side in range(CORES)]
        return [arrived[far, pair] for pair in chunk], places, picks

    crossed = {}

    def give_back(result, far, pair):
        back = far_hop(result, far, pair)
        crossed[far, pair] = [back[:1], hop(back[1:], 0, 0, 1)]

    size = CHUNK // CORES
    for far in range(1, groups):
        for first in range(0, pairs, size):
            chunk = list(range(first, min(pairs, first + size)))
            waiting, places, picks = crossing(far, chunk)
            depths = [CORES] * len(chunk)
            results = attend(waiting, picks, depths, ranks(places), key_blocks, key_rank)
            for pair, result in zip(chunk, results):
                give_back(result, far, pair)
    direct = [None] * CORES
    for first in range(0, pairs, size):
        chunk = list(range(max(first, 1), min(pairs, first + size)))
        waiting, places, picks = crossing(0, chunk)
        depths = [CORES] * len(chunk)
        if first == 0:
            depths += [1] * CORES
            picks += [(len(chunk) + step, len(tensors)) for step in range(CORES)]
            places += [(0, step, 0) for step in range(CORES)]
            waiting = waiting + [keys[step, 0] for step in range(CORES)]
        results = attend(waiting, picks, depths, ranks(places), key_blocks, key_rank)
        for pair, result in zip(chunk, results):
            give_back(result, 0, pair)
        for step, result in enumerate(results[len(chunk) :]):
            direct[step] = hop(result, 0, step)
    first = direct + [one for far in range(1, groups) for one in crossed[far, 0]]
    rest = [
        one for pair in range(1, pairs) for far in range(groups) for one in crossed[far, pair]
    ]
    chosen = list(range(1, pairs))
    merged = merge(where, rest, chosen, groups, members, rows, heads)
    return merge(where, first, [0], groups, members, rows, heads, merged)


def solution(mesh):
    placed = (P(("groups", "tok"), None),) * 5 + (P("groups"),) * 2
    return jax.shard_map(
        shards, mesh=mesh, in_specs=placed, out_specs=P(("groups", "tok"), None), check_vma=False
    )
```

```python
import functools
import math

import jax
import jax.numpy as jnp
from jax import lax
from jax.experimental import pallas as pl
from jax.experimental.pallas import tpu as pltpu
from jax.sharding import PartitionSpec as P

HEADS = 16
HEAD_DIM = 128
CORES = 2
STAT_ROWS = 16
STAT_TERMS = 4
CHUNK = 4
VMEM_LIMIT = 48 * 1024 * 1024
VMEM_WHOLE = 63 * 1024 * 1024


def token_ranks(positions, patch_starts, order_starts):
    patch_count = patch_starts.shape[0]
    slot_ids = jnp.arange(patch_count, dtype=jnp.int32)
    patch_of = jnp.sum((patch_starts[None, :] <= positions[:, None]).astype(jnp.int32), axis=1) - 1
    matches = (order_starts[:, None] == patch_starts[None, :]).astype(jnp.int32)
    rank_of = jnp.sum(matches * slot_ids[:, None], axis=0)
    one_hot = (patch_of[:, None] == slot_ids[None, :]).astype(jnp.int32)
    return jnp.sum(one_hot * rank_of[None, :], axis=1)


def split_kernel(members, width, where, queries, *rest):
    kinds = 4
    tensors, outs = rest[:kinds], rest[kinds : kinds + members + 2]
    whole_room, near_room, far_room, into, out_of = rest[kinds + members + 2 :]
    member, core = where[0] // CORES % members, where[0] % CORES
    arriving = [
        pltpu.make_async_copy(src, whole_room.at[i], into.at[i])
        for i, src in enumerate(tensors + (queries,))
    ]
    for copy in arriving[::-1]:
        copy.start()

    def columns(step):
        return pl.ds(pl.multiple_of((member ^ step) * width, width), width)

    leaving = []

    def send(room, out):
        leaving.append(pltpu.make_async_copy(room, out, out_of.at[len(leaving)]))
        leaving[-1].start()

    arriving[kinds].wait()
    for side in range(CORES)[::-1]:
        for pair in range(members // CORES):
            picked = columns(pair * CORES + (core ^ side))
            far_room[side, pair] = whole_room[kinds, :, picked]
        send(far_room.at[side], outs[members + side])
    for copy in arriving[:kinds]:
        copy.wait()
    for step in range(members)[::-1]:
        depth = outs[step].shape[0]
        for kind in range(depth):
            near_room[step, kind] = whole_room[kind, :, columns(step)]
        send(near_room.at[step, pl.ds(0, depth)], outs[step])
    for copy in leaving:
        copy.wait()


def split_columns(where, members, queries, tensors):
    rows, columns = queries.shape
    width = columns // members
    kinds = len(tensors) + 1
    near = (kinds, rows, width)
    far = (members // CORES, rows, width)
    anywhere = pl.BlockSpec(memory_space=pl.ANY)
    size = kinds * rows * columns * 2
    result = pl.pallas_call(
        functools.partial(split_kernel, members, width),
        out_shape=[jax.ShapeDtypeStruct(near, queries.dtype)] * CORES
        + [jax.ShapeDtypeStruct((kinds - 1,) + near[1:], queries.dtype)] * (members - CORES)
        + [jax.ShapeDtypeStruct(far, queries.dtype)] * CORES,
        in_specs=[pl.BlockSpec(memory_space=pltpu.SMEM)] + [anywhere] * kinds,
        out_specs=[anywhere] * (members + CORES),
        scratch_shapes=[
            pltpu.VMEM((kinds, rows, columns), queries.dtype),
            pltpu.VMEM((members,) + near, queries.dtype),
            pltpu.VMEM((CORES,) + far, queries.dtype),
            pltpu.SemaphoreType.DMA((kinds,)),
            pltpu.SemaphoreType.DMA((members + CORES,)),
        ],
        compiler_params=pltpu.CompilerParams(vmem_limit_bytes=VMEM_WHOLE),
        cost_estimate=pl.CostEstimate(flops=0, bytes_accessed=2 * size, transcendentals=0),
        name="split_columns",
    )(where, queries, *tensors)
    return result[:members], result[members:]


def attend_kernel(picks, arrays, blocks, heads, key_rank, query_rank, *refs):
    queries = [refs[array].at[at] for array, at in picks]
    keys, outs = refs[arrays : arrays + blocks], refs[arrays + blocks :]
    places = [out.at[at] for out in outs for at in range(out.shape[0])]
    rows = queries[0].shape[0]
    dims = (((1,), (1,)), ((), ()))
    scale = math.log2(math.e) / math.sqrt(HEAD_DIM)
    fresh_ok = key_rank[...] <= query_rank[...]
    lane = lax.broadcasted_iota(jnp.int32, (len(picks) * rows, HEAD_DIM), 1)
    kept = jnp.zeros((len(picks) * rows, HEAD_DIM), jnp.float32)
    for head in range(heads):
        columns = slice(head * HEAD_DIM, (head + 1) * HEAD_DIM)
        query = jnp.concatenate([ref[:, columns] for ref in queries], axis=0)
        fresh_keys, fresh_values, stale_keys, stale_values = (
            jnp.concatenate([ref[kind, :, columns] for ref in keys], axis=0) for kind in range(4)
        )
        fresh = lax.dot_general(query, fresh_keys, dims, preferred_element_type=jnp.float32)
        stale = lax.dot_general(query, stale_keys, dims, preferred_element_type=jnp.float32)
        scores = jnp.where(fresh_ok, fresh, stale)
        row_max = jnp.max(scores, axis=1, keepdims=True)
        weights = jnp.exp2((scores - row_max) * scale)
        total = jnp.sum(weights, axis=1, keepdims=True)
        fresh_weights = jnp.where(fresh_ok, weights, 0.0).astype(jnp.bfloat16)
        stale_weights = jnp.where(fresh_ok, 0.0, weights).astype(jnp.bfloat16)
        mixed = jnp.dot(fresh_weights, fresh_values, preferred_element_type=jnp.float32)
        mixed = mixed + jnp.dot(stale_weights, stale_values, preferred_element_type=jnp.float32)
        mixed = (mixed / total).astype(jnp.bfloat16)
        for i, place in enumerate(places):
            place[head * rows : (head + 1) * rows, :] = mixed[i * rows : (i + 1) * rows]
        level = row_max * scale + jnp.log2(total)
        high = level.astype(jnp.bfloat16).astype(jnp.float32)
        middle = (level - high).astype(jnp.bfloat16).astype(jnp.float32)
        for term, value in enumerate((high, middle, level - high - middle)):
            kept = jnp.where(lane == head * STAT_TERMS + term, value, kept)
    turned = kept.T[:STAT_ROWS]
    for i, place in enumerate(places):
        mine = turned[:, i * rows : (i + 1) * rows].astype(jnp.bfloat16)
        filler = jnp.zeros((STAT_ROWS, HEAD_DIM - rows), jnp.bfloat16)
        place[heads * rows :, :] = jnp.concatenate([mine, filler], axis=1)


def attend(arrays, picks, depths, query_rank, keys, key_rank):
    blocks = len(keys)
    rows, width = keys[0].shape[1:]
    heads = width // HEAD_DIM
    query_count, key_count = len(picks) * rows, blocks * rows
    vmem = pl.BlockSpec(memory_space=pltpu.VMEM)
    tile = (heads * rows + STAT_ROWS, HEAD_DIM)
    return pl.pallas_call(
        functools.partial(attend_kernel, picks, len(arrays), blocks, heads),
        out_shape=[jax.ShapeDtypeStruct((depth,) + tile, jnp.bfloat16) for depth in depths],
        in_specs=[vmem] * (2 + len(arrays) + blocks),
        out_specs=[vmem] * len(depths),
        compiler_params=pltpu.CompilerParams(vmem_limit_bytes=VMEM_LIMIT),
        cost_estimate=pl.CostEstimate(
            flops=8 * heads * query_count * key_count * HEAD_DIM,
            bytes_accessed=2 * width * (query_count * 2 + key_count * 4),
            transcendentals=heads * query_count * key_count,
        ),
        name="attend",
    )(key_rank[None, :], query_rank[:, None], *arrays, *keys)


def merge_kernel(chosen, parts, members, heads, where, *refs):
    out, room, sems = refs[-3:]
    rows = out.shape[0]
    width = heads * HEAD_DIM
    member, core = where[0] // CORES % members, where[0] % CORES
    refs = list(refs)
    leaving = []
    for place, pair in enumerate(chosen):
        direct = [refs.pop(0) for _ in range(CORES)] if pair == 0 else None
        crossed = [refs.pop(0) for _ in range((parts if pair else parts - 1) * CORES)]
        for side in range(CORES):
            group = [one.at[0][...] for one in crossed[side::CORES]]
            if pair == 0:
                one = direct[0].at[0][...]
                for step in range(1, CORES):
                    one = jnp.where((core ^ side) == step, direct[step].at[0][...], one)
                group.append(one)
            at = place * CORES + side
            levels = [one[heads * rows :].astype(jnp.float32).T[:rows] for one in group]
            for head in range(heads):
                lane = head * STAT_TERMS
                level = [
                    one[:, lane : lane + 1]
                    + one[:, lane + 1 : lane + 2]
                    + one[:, lane + 2 : lane + 3]
                    for one in levels
                ]
                top = functools.reduce(jnp.maximum, level)
                shares = [jnp.exp2(one - top) for one in level]
                total = functools.reduce(jnp.add, shares)
                mixed = functools.reduce(
                    jnp.add,
                    [
                        one[head * rows : (head + 1) * rows].astype(jnp.float32) * (share / total)
                        for one, share in zip(group, shares)
                    ],
                )
                room[at, :, head * HEAD_DIM : (head + 1) * HEAD_DIM] = mixed.astype(out.dtype)
            start = pl.multiple_of((member ^ (pair * CORES + (core ^ side))) * width, width)
            columns = out.at[:, pl.ds(start, width)]
            leaving.append(pltpu.make_async_copy(room.at[at], columns, sems.at[at]))
            leaving[-1].start()
    for copy in leaving:
        copy.wait()


def merge(where, partials, chosen, parts, members, rows, heads, earlier=None):
    vmem, anywhere = pl.BlockSpec(memory_space=pltpu.VMEM), pl.BlockSpec(memory_space=pl.ANY)
    blocks = len(chosen) * CORES
    operands = [where] + partials + ([] if earlier is None else [earlier])
    specs = [pl.BlockSpec(memory_space=pltpu.SMEM)] + [vmem] * len(partials)
    return pl.pallas_call(
        functools.partial(merge_kernel, chosen, parts, members, heads),
        out_shape=jax.ShapeDtypeStruct((rows, members * heads * HEAD_DIM), jnp.bfloat16),
        in_specs=specs + ([] if earlier is None else [anywhere]),
        out_specs=anywhere,
        scratch_shapes=[
            pltpu.VMEM((blocks, rows, heads * HEAD_DIM), jnp.bfloat16),
            pltpu.SemaphoreType.DMA((blocks,)),
        ],
        input_output_aliases={} if earlier is None else {len(operands) - 1: 0},
        compiler_params=pltpu.CompilerParams(vmem_limit_bytes=VMEM_LIMIT),
        name="merge",
    )(*operands)


def after(array, earlier):
    return lax.optimization_barrier((array, earlier))[0]


def shards(queries, fresh_keys, fresh_values, stale_keys, stale_values, patch_starts, order_starts):
    devices = lax.axis_size("tok")
    rows = queries.shape[0]
    chips = devices // CORES
    members = min(chips // 2, HEADS)
    groups = chips // members
    heads = HEADS // members
    me = lax.axis_index("tok")
    core, chip = me % CORES, me // CORES
    group, member = chip // members, chip % members
    where = me[None].astype(jnp.int32)
    pairs = members // CORES

    def hop(array, far, near, side=0):
        flip = (far * members + near) * CORES + side
        if flip == 0:
            return array
        return lax.ppermute(array, "tok", [(i, i ^ flip) for i in range(devices)])

    def far_hop(array, far, pair):
        flips = [(far * members + pair * CORES + i % CORES) * CORES for i in range(devices)]
        return lax.ppermute(array, "tok", [(i, i ^ flips[i]) for i in range(devices)])

    def ranks(places):
        spots = [
            (((group ^ far) * members + (member ^ near)) * CORES + (core ^ side)) * rows
            + jnp.arange(rows, dtype=jnp.int32)
            for far, near, side in places
        ]
        return token_ranks(jnp.concatenate(spots), starts_later, order_starts)

    tensors = (fresh_keys, fresh_values, stale_keys, stale_values)
    blocks, (mine, others) = split_columns(where, members, queries, tensors)
    order = list(range(members))[::-1]
    other_mine = hop(others, 0, 0, 1)
    payload = [jnp.stack([mine[pair], other_mine[pair]]) for pair in range(pairs)]
    arrived = {
        (far, pair): far_hop(payload[pair], far, pair)
        for far in range(1, groups)
        for pair in range(pairs)[::-1]
    }
    first_far = arrived[1, 0]
    for pair in range(1, pairs):
        arrived[0, pair] = far_hop(payload[pair], 0, pair)
    keys = {}
    keys[0, 0] = blocks[0]
    keys[0, 1] = hop(after(blocks[0], other_mine), 0, 0, 1)
    for near in order[:-1]:
        keys[near, 0] = hop(blocks[near], 0, near)
        keys[near, 1] = hop(after(keys[near, 0], first_far), 0, 0, 1)
    starts_later = after(patch_starts, keys[order[0], 0])
    key_rank = ranks([(0, near, side) for near in range(members) for side in range(CORES)])
    key_blocks = [keys[near, side] for near in range(members) for side in range(CORES)]

    def crossing(far, chunk):
        places = [(far, pair * CORES + core, side) for pair in chunk for side in range(CORES)]
        picks = [(at, side) for at in range(len(chunk)) for side in range(CORES)]
        return [arrived[far, pair] for pair in chunk], places, picks

    crossed = {}

    def give_back(result, far, pair):
        back = far_hop(result, far, pair)
        crossed[far, pair] = [back[:1], hop(back[1:], 0, 0, 1)]

    size = CHUNK // CORES
    for far in range(1, groups):
        for first in range(0, pairs, size):
            chunk = list(range(first, min(pairs, first + size)))
            waiting, places, picks = crossing(far, chunk)
            depths = [CORES] * len(chunk)
            results = attend(waiting, picks, depths, ranks(places), key_blocks, key_rank)
            for pair, result in zip(chunk, results):
                give_back(result, far, pair)
    direct = [None] * CORES
    for first in range(0, pairs, size):
        chunk = list(range(max(first, 1), min(pairs, first + size)))
        waiting, places, picks = crossing(0, chunk)
        depths = [CORES] * len(chunk)
        if first == 0:
            depths += [1] * CORES
            picks += [(len(chunk) + step, len(tensors)) for step in range(CORES)]
            places += [(0, step, 0) for step in range(CORES)]
            waiting = waiting + [keys[step, 0] for step in range(CORES)]
        results = attend(waiting, picks, depths, ranks(places), key_blocks, key_rank)
        for pair, result in zip(chunk, results):
            give_back(result, 0, pair)
        for step, result in enumerate(results[len(chunk) :]):
            direct[step] = hop(result, 0, step)
    first = direct + [one for far in range(1, groups) for one in crossed[far, 0]]
    rest = [
        one for pair in range(1, pairs) for far in range(groups) for one in crossed[far, pair]
    ]
    chosen = list(range(1, pairs))
    merged = merge(where, rest, chosen, groups, members, rows, heads)
    return merge(where, first, [0], groups, members, rows, heads, merged)


def solution(mesh):
    placed = (P(("groups", "tok"), None),) * 5 + (P("groups"),) * 2
    return jax.shard_map(
        shards, mesh=mesh, in_specs=placed, out_specs=P(("groups", "tok"), None), check_vma=False
    )
```

```python
import functools
import math

import jax
import jax.numpy as jnp
from jax import lax
from jax.experimental import pallas as pl
from jax.experimental.pallas import tpu as pltpu
from jax.sharding import PartitionSpec as P

HEADS = 16
HEAD_DIM = 128
CORES = 2
STAT_ROWS = 16
STAT_TERMS = 4
CHUNK = 4
VMEM_LIMIT = 48 * 1024 * 1024
VMEM_WHOLE = 63 * 1024 * 1024


def token_ranks(positions, patch_starts, order_starts):
    patch_count = patch_starts.shape[0]
    slot_ids = jnp.arange(patch_count, dtype=jnp.int32)
    patch_of = jnp.sum((patch_starts[None, :] <= positions[:, None]).astype(jnp.int32), axis=1) - 1
    matches = (order_starts[:, None] == patch_starts[None, :]).astype(jnp.int32)
    rank_of = jnp.sum(matches * slot_ids[:, None], axis=0)
    one_hot = (patch_of[:, None] == slot_ids[None, :]).astype(jnp.int32)
    return jnp.sum(one_hot * rank_of[None, :], axis=1)


def split_kernel(members, width, where, queries, *rest):
    kinds = 4
    tensors, outs = rest[:kinds], rest[kinds : kinds + members + 2]
    whole_room, near_room, far_room, into, out_of = rest[kinds + members + 2 :]
    member, core = where[0] // CORES % members, where[0] % CORES
    arriving = [
        pltpu.make_async_copy(src, whole_room.at[i], into.at[i])
        for i, src in enumerate(tensors + (queries,))
    ]
    for copy in arriving[::-1]:
        copy.start()

    def columns(step):
        return pl.ds(pl.multiple_of((member ^ step) * width, width), width)

    leaving = []

    def send(room, out):
        leaving.append(pltpu.make_async_copy(room, out, out_of.at[len(leaving)]))
        leaving[-1].start()

    arriving[kinds].wait()
    for side in range(CORES)[::-1]:
        for pair in range(members // CORES):
            picked = columns(pair * CORES + (core ^ side))
            far_room[side, pair] = whole_room[kinds, :, picked]
        send(far_room.at[side], outs[members + side])
    for copy in arriving[:kinds]:
        copy.wait()
    for step in range(members)[::-1]:
        depth = outs[step].shape[0]
        for kind in range(depth):
            near_room[step, kind] = whole_room[kind, :, columns(step)]
        send(near_room.at[step, pl.ds(0, depth)], outs[step])
    for copy in leaving:
        copy.wait()


def split_columns(where, members, queries, tensors):
    rows, columns = queries.shape
    width = columns // members
    kinds = len(tensors) + 1
    near = (kinds, rows, width)
    far = (members // CORES, rows, width)
    anywhere = pl.BlockSpec(memory_space=pl.ANY)
    size = kinds * rows * columns * 2
    result = pl.pallas_call(
        functools.partial(split_kernel, members, width),
        out_shape=[jax.ShapeDtypeStruct(near, queries.dtype)] * CORES
        + [jax.ShapeDtypeStruct((kinds - 1,) + near[1:], queries.dtype)] * (members - CORES)
        + [jax.ShapeDtypeStruct(far, queries.dtype)] * CORES,
        in_specs=[pl.BlockSpec(memory_space=pltpu.SMEM)] + [anywhere] * kinds,
        out_specs=[anywhere] * (members + CORES),
        scratch_shapes=[
            pltpu.VMEM((kinds, rows, columns), queries.dtype),
            pltpu.VMEM((members,) + near, queries.dtype),
            pltpu.VMEM((CORES,) + far, queries.dtype),
            pltpu.SemaphoreType.DMA((kinds,)),
            pltpu.SemaphoreType.DMA((members + CORES,)),
        ],
        compiler_params=pltpu.CompilerParams(vmem_limit_bytes=VMEM_WHOLE),
        cost_estimate=pl.CostEstimate(flops=0, bytes_accessed=2 * size, transcendentals=0),
        name="split_columns",
    )(where, queries, *tensors)
    return result[:members], result[members:]


def attend_kernel(picks, arrays, blocks, heads, key_rank, query_rank, *refs):
    queries = [refs[array].at[at] for array, at in picks]
    keys, outs = refs[arrays : arrays + blocks], refs[arrays + blocks :]
    places = [out.at[at] for out in outs for at in range(out.shape[0])]
    rows = queries[0].shape[0]
    dims = (((1,), (1,)), ((), ()))
    scale = math.log2(math.e) / math.sqrt(HEAD_DIM)
    fresh_ok = key_rank[...] <= query_rank[...]
    lane = lax.broadcasted_iota(jnp.int32, (len(picks) * rows, HEAD_DIM), 1)
    kept = jnp.zeros((len(picks) * rows, HEAD_DIM), jnp.float32)
    for head in range(heads):
        columns = slice(head * HEAD_DIM, (head + 1) * HEAD_DIM)
        query = jnp.concatenate([ref[:, columns] for ref in queries], axis=0)
        fresh_keys, fresh_values, stale_keys, stale_values = (
            jnp.concatenate([ref[kind, :, columns] for ref in keys], axis=0) for kind in range(4)
        )
        fresh = lax.dot_general(query, fresh_keys, dims, preferred_element_type=jnp.float32)
        stale = lax.dot_general(query, stale_keys, dims, preferred_element_type=jnp.float32)
        scores = jnp.where(fresh_ok, fresh, stale)
        row_max = jnp.max(scores, axis=1, keepdims=True)
        weights = jnp.exp2((scores - row_max) * scale)
        total = jnp.sum(weights, axis=1, keepdims=True)
        fresh_weights = jnp.where(fresh_ok, weights, 0.0).astype(jnp.bfloat16)
        stale_weights = jnp.where(fresh_ok, 0.0, weights).astype(jnp.bfloat16)
        mixed = jnp.dot(fresh_weights, fresh_values, preferred_element_type=jnp.float32)
        mixed = mixed + jnp.dot(stale_weights, stale_values, preferred_element_type=jnp.float32)
        mixed = (mixed / total).astype(jnp.bfloat16)
        for i, place in enumerate(places):
            place[head * rows : (head + 1) * rows, :] = mixed[i * rows : (i + 1) * rows]
        level = row_max * scale + jnp.log2(total)
        high = level.astype(jnp.bfloat16).astype(jnp.float32)
        middle = (level - high).astype(jnp.bfloat16).astype(jnp.float32)
        for term, value in enumerate((high, middle, level - high - middle)):
            kept = jnp.where(lane == head * STAT_TERMS + term, value, kept)
    turned = kept.T[:STAT_ROWS]
    for i, place in enumerate(places):
        mine = turned[:, i * rows : (i + 1) * rows].astype(jnp.bfloat16)
        filler = jnp.zeros((STAT_ROWS, HEAD_DIM - rows), jnp.bfloat16)
        place[heads * rows :, :] = jnp.concatenate([mine, filler], axis=1)


def attend(arrays, picks, depths, query_rank, keys, key_rank):
    blocks = len(keys)
    rows, width = keys[0].shape[1:]
    heads = width // HEAD_DIM
    query_count, key_count = len(picks) * rows, blocks * rows
    vmem = pl.BlockSpec(memory_space=pltpu.VMEM)
    tile = (heads * rows + STAT_ROWS, HEAD_DIM)
    return pl.pallas_call(
        functools.partial(attend_kernel, picks, len(arrays), blocks, heads),
        out_shape=[jax.ShapeDtypeStruct((depth,) + tile, jnp.bfloat16) for depth in depths],
        in_specs=[vmem] * (2 + len(arrays) + blocks),
        out_specs=[vmem] * len(depths),
        compiler_params=pltpu.CompilerParams(vmem_limit_bytes=VMEM_LIMIT),
        cost_estimate=pl.CostEstimate(
            flops=8 * heads * query_count * key_count * HEAD_DIM,
            bytes_accessed=2 * width * (query_count * 2 + key_count * 4),
            transcendentals=heads * query_count * key_count,
        ),
        name="attend",
    )(key_rank[None, :], query_rank[:, None], *arrays, *keys)


def merge_kernel(chosen, parts, members, heads, where, *refs):
    out, room, sems = refs[-3:]
    rows = out.shape[0]
    width = heads * HEAD_DIM
    member, core = where[0] // CORES % members, where[0] % CORES
    refs = list(refs)
    leaving = []
    for place, pair in enumerate(chosen):
        direct = [refs.pop(0) for _ in range(CORES)] if pair == 0 else None
        crossed = [refs.pop(0) for _ in range((parts if pair else parts - 1) * CORES)]
        for side in range(CORES):
            group = [one.at[0][...] for one in crossed[side::CORES]]
            if pair == 0:
                one = direct[0].at[0][...]
                for step in range(1, CORES):
                    one = jnp.where((core ^ side) == step, direct[step].at[0][...], one)
                group.append(one)
            at = place * CORES + side
            levels = [one[heads * rows :].astype(jnp.float32).T[:rows] for one in group]
            for head in range(heads):
                lane = head * STAT_TERMS
                level = [
                    one[:, lane : lane + 1]
                    + one[:, lane + 1 : lane + 2]
                    + one[:, lane + 2 : lane + 3]
                    for one in levels
                ]
                top = functools.reduce(jnp.maximum, level)
                shares = [jnp.exp2(one - top) for one in level]
                total = functools.reduce(jnp.add, shares)
                mixed = functools.reduce(
                    jnp.add,
                    [
                        one[head * rows : (head + 1) * rows].astype(jnp.float32) * (share / total)
                        for one, share in zip(group, shares)
                    ],
                )
                room[at, :, head * HEAD_DIM : (head + 1) * HEAD_DIM] = mixed.astype(out.dtype)
            start = pl.multiple_of((member ^ (pair * CORES + (core ^ side))) * width, width)
            columns = out.at[:, pl.ds(start, width)]
            leaving.append(pltpu.make_async_copy(room.at[at], columns, sems.at[at]))
            leaving[-1].start()
    for copy in leaving:
        copy.wait()


def merge(where, partials, chosen, parts, members, rows, heads, earlier=None):
    vmem, anywhere = pl.BlockSpec(memory_space=pltpu.VMEM), pl.BlockSpec(memory_space=pl.ANY)
    blocks = len(chosen) * CORES
    operands = [where] + partials + ([] if earlier is None else [earlier])
    specs = [pl.BlockSpec(memory_space=pltpu.SMEM)] + [vmem] * len(partials)
    return pl.pallas_call(
        functools.partial(merge_kernel, chosen, parts, members, heads),
        out_shape=jax.ShapeDtypeStruct((rows, members * heads * HEAD_DIM), jnp.bfloat16),
        in_specs=specs + ([] if earlier is None else [anywhere]),
        out_specs=anywhere,
        scratch_shapes=[
            pltpu.VMEM((blocks, rows, heads * HEAD_DIM), jnp.bfloat16),
            pltpu.SemaphoreType.DMA((blocks,)),
        ],
        input_output_aliases={} if earlier is None else {len(operands) - 1: 0},
        compiler_params=pltpu.CompilerParams(vmem_limit_bytes=VMEM_LIMIT),
        name="merge",
    )(*operands)


def after(array, earlier):
    return lax.optimization_barrier((array, earlier))[0]


def shards(queries, fresh_keys, fresh_values, stale_keys, stale_values, patch_starts, order_starts):
    devices = lax.axis_size("tok")
    rows = queries.shape[0]
    chips = devices // CORES
    members = min(chips // 2, HEADS)
    groups = chips // members
    heads = HEADS // members
    me = lax.axis_index("tok")
    core, chip = me % CORES, me // CORES
    group, member = chip // members, chip % members
    where = me[None].astype(jnp.int32)
    pairs = members // CORES

    def hop(array, far, near, side=0):
        flip = (far * members + near) * CORES + side
        if flip == 0:
            return array
        return lax.ppermute(array, "tok", [(i, i ^ flip) for i in range(devices)])

    def far_hop(array, far, pair):
        flips = [(far * members + pair * CORES + i % CORES) * CORES for i in range(devices)]
        return lax.ppermute(array, "tok", [(i, i ^ flips[i]) for i in range(devices)])

    def ranks(places):
        spots = [
            (((group ^ far) * members + (member ^ near)) * CORES + (core ^ side)) * rows
            + jnp.arange(rows, dtype=jnp.int32)
            for far, near, side in places
        ]
        return token_ranks(jnp.concatenate(spots), starts_later, order_starts)

    tensors = (fresh_keys, fresh_values, stale_keys, stale_values)
    blocks, (mine, others) = split_columns(where, members, queries, tensors)
    order = list(range(members))[::-1]
    other_mine = hop(others, 0, 0, 1)
    payload = [jnp.stack([mine[pair], other_mine[pair]]) for pair in range(pairs)]
    arrived = {
        (far, pair): far_hop(payload[pair], far, pair)
        for far in range(1, groups)
        for pair in range(pairs)[::-1]
    }
    first_far = arrived[1, 0]
    for pair in range(1, pairs):
        arrived[0, pair] = far_hop(payload[pair], 0, pair)
    keys = {}
    keys[0, 0] = blocks[0]
    keys[0, 1] = hop(after(blocks[0], other_mine), 0, 0, 1)
    for near in order[:-1]:
        keys[near, 0] = hop(blocks[near], 0, near)
        keys[near, 1] = hop(after(after(keys[near, 0], first_far), keys[0, 1]), 0, 0, 1)
    starts_later = after(patch_starts, keys[order[0], 0])
    key_rank = ranks([(0, near, side) for near in range(members) for side in range(CORES)])
    key_blocks = [keys[near, side] for near in range(members) for side in range(CORES)]

    def crossing(far, chunk):
        places = [(far, pair * CORES + core, side) for pair in chunk for side in range(CORES)]
        picks = [(at, side) for at in range(len(chunk)) for side in range(CORES)]
        return [arrived[far, pair] for pair in chunk], places, picks

    crossed = {}

    def give_back(result, far, pair):
        back = far_hop(result, far, pair)
        crossed[far, pair] = [back[:1], hop(back[1:], 0, 0, 1)]

    size = CHUNK // CORES
    for far in range(1, groups):
        for first in range(0, pairs, size):
            chunk = list(range(first, min(pairs, first + size)))
            waiting, places, picks = crossing(far, chunk)
            depths = [CORES] * len(chunk)
            results = attend(waiting, picks, depths, ranks(places), key_blocks, key_rank)
            for pair, result in zip(chunk, results):
                give_back(result, far, pair)
    direct = [None] * CORES
    for first in range(0, pairs, size):
        chunk = list(range(max(first, 1), min(pairs, first + size)))
        waiting, places, picks = crossing(0, chunk)
        depths = [CORES] * len(chunk)
        if first == 0:
            depths += [1] * CORES
            picks += [(len(chunk) + step, len(tensors)) for step in range(CORES)]
            places += [(0, step, 0) for step in range(CORES)]
            waiting = waiting + [keys[step, 0] for step in range(CORES)]
        results = attend(waiting, picks, depths, ranks(places), key_blocks, key_rank)
        for pair, result in zip(chunk, results):
            give_back(result, 0, pair)
        for step, result in enumerate(results[len(chunk) :]):
            direct[step] = hop(result, 0, step)
    first = direct + [one for far in range(1, groups) for one in crossed[far, 0]]
    rest = [
        one for pair in range(1, pairs) for far in range(groups) for one in crossed[far, pair]
    ]
    chosen = list(range(1, pairs))
    merged = merge(where, rest, chosen, groups, members, rows, heads)
    return merge(where, first, [0], groups, members, rows, heads, merged)


def solution(mesh):
    placed = (P(("groups", "tok"), None),) * 5 + (P("groups"),) * 2
    return jax.shard_map(
        shards, mesh=mesh, in_specs=placed, out_specs=P(("groups", "tok"), None), check_vma=False
    )
```
